32 devices in a mesh: job: 2 (over x), col: 16 (over z, y, core).
Axes of the slice: x: 2, y: 2, z: 4, core: 2. Of those that a mesh axis runs over, the one named last changes fastest.
Arguments:
- tau_packed: bfloat16 [256, 1200], P(('job', 'col')), parts along dimension 0, may hold values from -6 to 6
- pair_irrep: int32 [256], P('job'), parts along dimension 0, may hold values from 0 to 7
- cd_sizes: int32 [16], P('job'), parts along dimension 0, may hold values from 1 to 1200, 3200 in all
- ab_sizes: int32 [16], P('job'), parts along dimension 0, may hold values from 1 to 6400, 25600 in all
- integrals: bfloat16 [6400, 25600], P('job', 'col'), parts along dimension 0, may hold values from -0.1875 to 0.1875
- occ_energy: float32 [256], P('job'), parts along dimension 0, may hold values from -2 to -0.5
- virt_energy: float32 [51200], P(('job', 'col')), parts along dimension 0, may hold values from 1 to 8
Outputs:
- update: float32 [256, 25600], P('job', 'col'), parts along dimension 0
- pair_energy: float32 [256], P('job'), parts along dimension 0
The draws below stay inside these ranges and needn't reach their ends.
There are 2 independent parts, one for each index of `job`. The reference program is written for one: setup_inputs(seed, part) draws one part's arguments, and reference() takes and returns one part's arrays. A program takes and returns all parts, laid end to end along the dimension named above; each array names one. Nothing has to cross between parts.
All inputs are finite; a program needn't handle non-finite values.
Results may differ from the reference program's by a relative error of at most 0.0003.
Values may be sent and summed in bfloat16 or wider, within the bound.
No kernel may reach another device: no remote copies, remote signals or barrier semaphores. Data moves between devices by JAX's collectives and lax.ppermute only.
A program may use at most 64 MiB of HBM per device.

```python
import math
import jax
import jax.numpy as jnp
import numpy as np

NIRR = 8
CD = 3200
CDMAX = 1200
P_SIZE = 128
AB = 25600
ABMAX = 6400


def draw_virt_energy(key, part):
    key = jax.random.fold_in(key, 5)
    fraction = jnp.arange(AB, dtype=jnp.float32) / AB
    base = jax.random.uniform(key, (AB,), jnp.float32, 1.0, 2.0)
    return base * (4.0 - 3.0 * fraction)


def set_ends(drawn, stream_key, low, largest):
    dims = drawn.shape
    index_at = [jax.random.randint(jax.random.fold_in(stream_key, axis), (), 0, dims[axis]) for axis in range(len(dims))]
    drawn = drawn.at[tuple(index_at)].set(low)
    longest = dims.index(max(dims))
    index_at[longest] = (index_at[longest] + 1) % dims[longest]
    return drawn.at[tuple(index_at)].set(largest)


def block_levels(own_key, extent, split, low, largest):
    def one(dim, blocks):
        heights = jax.random.uniform(jax.random.fold_in(jax.random.fold_in(own_key, 6), dim), (blocks,), jnp.float32, low / len(split), largest / len(split))
        return jnp.repeat(jnp.exp(heights), extent[dim] // blocks).reshape((-1,) + (1,) * (len(extent) - dim - 1))

    factor_of = one(*split[0])
    for cut in split[1:]:
        factor_of = factor_of * one(*cut)
    return factor_of


def length_profile(count, total, bound, lean):
    loads = [(1 << 20) // math.isqrt(standing ** lean) + 1 for standing in range(2, count + 1)]
    rest, given = total - bound - (count - 1), [1] * (count - 1)
    while rest > 0:
        candidates = [i for i in range(count - 1) if given[i] < bound]
        pool, left = sum([loads[i] for i in candidates]), rest
        for i in candidates:
            extra = min(bound - given[i], max(1, left * loads[i] // pool), rest)
            given[i] = given[i] + extra
            rest = rest - extra
    return np.array([bound] + given)


def ragged(rng, amount, total, reach, skew):
    if amount == 2:
        one = jax.random.randint(rng, (), max(1, total - reach), min(reach, total - 1) + 1)
        return jnp.stack([one, total - one])
    sizes = jnp.asarray(length_profile(amount, total, reach, skew), jnp.int32)
    couples = (amount - 1) // 2
    giver, taker = sizes[1:1 + 2 * couples:2], sizes[2:2 + 2 * couples:2]
    margin = jnp.minimum(giver - 1, reach - taker)
    moved = jax.random.randint(jax.random.fold_in(rng, 1), (couples,), 0, 1 << 20) % (margin + 1)
    sizes = sizes.at[1:1 + 2 * couples:2].set(giver - moved).at[2:2 + 2 * couples:2].set(taker + moved)
    return sizes[jax.random.permutation(jax.random.fold_in(rng, 2), amount)]


def bell_draw(stream_key, extent, scale, most, shards=(), kind=jnp.bfloat16):
    drawn = jax.random.normal(stream_key, extent, jnp.float32) * scale
    if len(shards) > 0:
        drawn = block_levels(stream_key, extent, shards, -0.22, 0.18) * drawn
    return jnp.clip(drawn, min=-most, max=most).astype(kind)


def setup_inputs(seed: int = 0, part: int = 0) -> dict:
    splits = jax.random.split(jax.random.key(seed), 8)
    part_splits = jax.random.split(jax.random.fold_in(splits[7], part), 8)
    tau_packed = bell_draw(part_splits[0], (P_SIZE, CDMAX), 1.0, 6.0, ((0, 16),))
    pair_irrep = set_ends(jax.random.randint(part_splits[1], (P_SIZE,), 0, NIRR), jax.random.fold_in(part_splits[1], 1), 0, NIRR - 1).astype(jnp.int32)
    cd_sizes = ragged(part_splits[2], NIRR, CD, CDMAX, 2).astype(jnp.int32)
    ab_sizes = ragged(part_splits[3], NIRR, AB, ABMAX, 2).astype(jnp.int32)
    integrals = bell_draw(part_splits[4], (CD, AB), CDMAX ** -0.5, 0.1875, ((1, 16),))
    occ_energy = jnp.clip(jax.random.uniform(part_splits[5], (P_SIZE,), jnp.float32, -2.0, -0.5), -2.0, -0.5)
    virt_energy = draw_virt_energy(jax.random.fold_in(jax.random.fold_in(splits[7], part), 71), part)
    return {"tau_packed": tau_packed, "pair_irrep": pair_irrep, "cd_sizes": cd_sizes, "ab_sizes": ab_sizes, "integrals": integrals, "occ_energy": occ_energy, "virt_energy": virt_energy}


def expand(packed, irreps, cd_sizes, total_rows):
    starts = jnp.cumsum(cd_sizes) - cd_sizes
    labels = jnp.arange(cd_sizes.shape[0], dtype=jnp.int32)
    onehot = (irreps[:, None] == labels[None, :]).astype(jnp.int32)
    row_start = jnp.sum(onehot * starts[None, :], axis=1)
    row_size = jnp.sum(onehot * cd_sizes[None, :], axis=1)
    position = jnp.arange(total_rows, dtype=jnp.int32)[None, :] - row_start[:, None]
    valid = (position >= 0) & (position < row_size[:, None])
    clipped = jnp.clip(position, 0, packed.shape[1] - 1).astype(jnp.int32)
    values = jnp.take_along_axis(packed, clipped, axis=1)
    return jnp.where(valid, values, jnp.zeros_like(values))


def reference(tau_packed, pair_irrep, cd_sizes, ab_sizes, integrals, occ_energy, virt_energy):
    dense = expand(tau_packed, pair_irrep, cd_sizes, CD)
    column = jnp.arange(AB, dtype=jnp.int32)
    col_irrep = jnp.sum((column[:, None] >= jnp.cumsum(ab_sizes)[None, :]).astype(jnp.int32), axis=1)
    product = jnp.dot(dense, integrals, preferred_element_type=jnp.float32)
    ladder = jnp.where(pair_irrep[:, None] == col_irrep[None, :], product, jnp.zeros_like(product))
    denom = virt_energy[None, :] - occ_energy[:, None]
    update = ladder / denom
    pair_energy = jnp.sum(ladder * update, axis=1) / AB
    return update, pair_energy
```

```python
import functools
import jax
import jax.numpy as jnp
from jax import lax
from jax.experimental import pallas as pl
from jax.experimental.pallas import tpu as pltpu
from jax.sharding import PartitionSpec as P

LANES = 128
F32 = jnp.float32
I32 = jnp.int32


def generators(count):
    bits = count.bit_length() - 1
    return [(1 << b) | 1 for b in range(bits - 1, 0, -1)] + ([1] if bits else [])


def swap(value, key, count):
    return lax.ppermute(value, "col", [(i, i ^ key) for i in range(count)])


def ceil_lanes(extent):
    return -(-extent // LANES) * LANES


def setup_kernel(count, rows, ab_ref, irrep_ref, occ_ref, virt_ref, weight_ref, order_ref, label_ref):
    me = lax.axis_index("col")
    pairs = irrep_ref.shape[1]
    cols = weight_ref.shape[0]
    label = irrep_ref[...]
    low = jnp.zeros((1, pairs), I32)
    high = jnp.zeros((1, pairs), I32)
    start = -me * cols
    for g in range(ab_ref.shape[0]):
        end = start + ab_ref[g]
        low = jnp.where(label == g, start, low)
        high = jnp.where(label == g, end, high)
        start = end
    occ = occ_ref[...]
    for c in range(0, cols, LANES):
        width = min(LANES, cols - c)
        spread = jnp.broadcast_to(virt_ref[:, c:c + width], (LANES, width))
        virt = jnp.transpose(spread)
        at = c + lax.broadcasted_iota(I32, (width, LANES), 0)
        for p in range(0, pairs, LANES):
            lanes = slice(p, p + LANES)
            keep = (at >= low[:, lanes]) & (at < high[:, lanes])
            weight_ref[c:c + width, lanes] = jnp.where(keep, 1.0 / (virt - occ[:, lanes]), 0.0)
    source = lax.broadcasted_iota(I32, (1, pairs), 1)
    block = source // rows
    owner = jnp.full((1, pairs), me, I32)
    for step, key in enumerate(generators(count)):
        owner = owner ^ jnp.where((block >> step) & 1 == 1, key, 0)
    place = owner * rows + (source - block * rows)
    mine = lax.broadcasted_iota(I32, (pairs, pairs), 0)
    order_ref[...] = jnp.where(mine == place, 1.0, 0.0).astype(order_ref.dtype)
    for p in range(0, pairs, LANES):
        label_ref[p:p + LANES, :] = jnp.transpose(jnp.broadcast_to(label[:, p:p + LANES].astype(F32), (LANES, LANES)))


def ladder_kernel(
    total, tile, cd_ref, ab_ref, first_ref, second_ref, integrals_ref, weight_ref, order_ref, label_ref,
    update_ref, energy_ref, tau_ref, dense_ref,
):
    me = lax.axis_index("col")
    cols, cd_rows = integrals_ref.shape
    pairs = order_ref.shape[0]
    half, width = first_ref.shape
    window = tau_ref.shape[1]
    irreps = cd_ref.shape[0]
    tau_ref[:, :width] = jnp.dot(
        order_ref[:, :half], first_ref[...], preferred_element_type=F32
    ) + jnp.dot(order_ref[:, half:], second_ref[...], preferred_element_type=F32)
    dense_ref[:, :cd_rows] = jnp.zeros((pairs, cd_rows), dense_ref.dtype)
    lane = lax.broadcasted_iota(I32, (1, window), 1)

    def spread(g, starts):
        cd_start, ab_start = starts
        cd_end, ab_end = cd_start + cd_ref[g], ab_start + ab_ref[g]

        @pl.when((ab_end > 0) & (ab_start < cols))
        def _():
            shift = lax.rem(cd_start, LANES)
            base = pl.multiple_of(cd_start - shift, LANES)
            moved = pltpu.roll(tau_ref[...], shift, 1)
            valid = (lane >= shift) & (lane < shift + cd_ref[g])
            here = label_ref[:, :1] == g.astype(F32)
            old = dense_ref[:, pl.ds(base, window)]
            dense_ref[:, pl.ds(base, window)] = jnp.where(valid & here, moved, old.astype(F32)).astype(old.dtype)

        return cd_end, ab_end

    lax.fori_loop(0, irreps, spread, (jnp.int32(0), -me * cols))

    sizes = [s for s in (256, 512, 768, 1024, 1280, 1408, 2048) if s < cd_rows] + [cd_rows]
    sums = jnp.zeros((1, pairs), F32)
    energy_ref[...] = sums
    for t in range(0, cols, tile):
        cd_start, ab_start = jnp.int32(0), -me * cols
        begin, end = jnp.int32(0), jnp.int32(0)
        for g in range(irreps):
            cd_end, ab_end = cd_start + cd_ref[g], ab_start + ab_ref[g]
            begin = jnp.where(ab_end <= t, cd_end, begin)
            end = jnp.where(ab_start < t + tile, cd_end, end)
            cd_start, ab_start = cd_end, ab_end
        base = begin - lax.rem(begin, LANES)
        need = end - base
        below = 0
        for size in sizes:
            @pl.when((need > below) & (need <= size))
            def _(size=size):
                at = pl.multiple_of(jnp.minimum(base, cd_rows - size), LANES)
                ladder = lax.dot_general(
                    integrals_ref[t:t + tile, pl.ds(at, size)],
                    dense_ref[:, pl.ds(at, size)],
                    (((1,), (1,)), ((), ())),
                    preferred_element_type=F32,
                )
                update = ladder * weight_ref[t:t + tile, :]
                update_ref[t:t + tile, :] = update
                energy_ref[...] += jnp.sum(ladder * update, axis=0, keepdims=True)
            below = size
    energy_ref[...] = energy_ref[...] / total


def shards(tau_packed, pair_irrep, cd_sizes, ab_sizes, integrals, occ_energy, virt_energy):
    cd_rows, cols = integrals.shape
    rows, width = tau_packed.shape
    pairs = pair_irrep.shape[0]
    count = lax.axis_size("col")
    keys = generators(count)
    held = tau_packed
    for key in keys[:-1]:
        held = jnp.concatenate([held, swap(held, key, count)], axis=0)
    last = swap(held, keys[-1], count)

    vmem = pl.BlockSpec(memory_space=pltpu.VMEM)
    smem = pl.BlockSpec(memory_space=pltpu.SMEM)
    weight, order, label = pl.pallas_call(
        functools.partial(setup_kernel, count, rows),
        out_shape=(
            jax.ShapeDtypeStruct((cols, pairs), F32),
            jax.ShapeDtypeStruct((pairs, pairs), jnp.bfloat16),
            jax.ShapeDtypeStruct((pairs, LANES), F32),
        ),
        in_specs=[smem, vmem, vmem, vmem],
        out_specs=(vmem, vmem, vmem),
        cost_estimate=pl.CostEstimate(flops=10 * cols * pairs, bytes_accessed=4 * cols * pairs, transcendentals=0),
    )(ab_sizes, pair_irrep.reshape(1, pairs), occ_energy.reshape(1, pairs), virt_energy.reshape(1, cols))

    tile = 320 if cols % 320 == 0 else cols
    window = ceil_lanes(width + LANES - 1)
    turned = pltpu.with_memory_space_constraint(integrals.T, pltpu.VMEM)
    update, energy = pl.pallas_call(
        functools.partial(ladder_kernel, cols * count, tile),
        out_shape=(jax.ShapeDtypeStruct((cols, pairs), F32), jax.ShapeDtypeStruct((1, pairs), F32)),
        in_specs=[smem, smem] + [vmem] * 6,
        out_specs=(vmem, vmem),
        scratch_shapes=[pltpu.VMEM((pairs, window), F32), pltpu.VMEM((pairs, cd_rows + window), jnp.bfloat16)],
        compiler_params=pltpu.CompilerParams(vmem_limit_bytes=24 * 1024 * 1024),
        cost_estimate=pl.CostEstimate(
            flops=2 * cols * width * pairs, bytes_accessed=2 * cols * width + 4 * cols * pairs, transcendentals=0
        ),
    )(cd_sizes, ab_sizes, held, last, turned, weight, order, label)
    for key in keys:
        energy = energy + swap(energy, key, count)
    return update.T, energy.reshape(pairs)


def solution(mesh):
    placed = (
        P(("job", "col"), None),
        P("job"),
        P("job"),
        P("job"),
        P("job", "col"),
        P("job"),
        P(("job", "col")),
    )
    return jax.shard_map(
        shards, mesh=mesh, in_specs=placed, out_specs=(P("job", "col"), P("job")), check_vma=False
    )
```

```python
import functools
import jax
import jax.numpy as jnp
from jax import lax
from jax.experimental import pallas as pl
from jax.experimental.pallas import tpu as pltpu
from jax.sharding import PartitionSpec as P

LANES = 128
F32 = jnp.float32
I32 = jnp.int32


def generators(count):
    bits = count.bit_length() - 1
    return [(1 << b) | 1 for b in range(bits - 1, 0, -1)] + ([1] if bits else [])


def swap(value, key, count):
    return lax.ppermute(value, "col", [(i, i ^ key) for i in range(count)])


def ceil_lanes(extent):
    return -(-extent // LANES) * LANES


def window_sizes(cd_rows):
    return [size for size in (256, 512, 768, 1024, 1280, 1408, 2048) if size < cd_rows] + [cd_rows]


def windows(cd_ref, ab_ref, me, cols, tile, cd_rows):
    found = []
    for t in range(0, cols, tile):
        cd_start, ab_start = jnp.int32(0), -me * cols
        begin, end = jnp.int32(0), jnp.int32(0)
        for g in range(cd_ref.shape[0]):
            cd_end, ab_end = cd_start + cd_ref[g], ab_start + ab_ref[g]
            begin = jnp.where(ab_end <= t, cd_end, begin)
            end = jnp.where(ab_start < t + tile, cd_end, end)
            cd_start, ab_start = cd_end, ab_end
        base = begin - lax.rem(begin, LANES)
        size = jnp.int32(cd_rows)
        for choice in reversed(window_sizes(cd_rows)):
            size = jnp.where(end - base <= choice, choice, size)
        found.append((jnp.minimum(base, cd_rows - size), size))
    return found


def copy_kernel(source_ref, result_ref):
    result_ref[...] = source_ref[...]


def setup_kernel(
    count, rows, tile, cd_hbm, ab_hbm, irrep_hbm, occ_hbm, virt_ref, integrals_ref,
    weight_ref, order_ref, label_ref, packed_ref, table_ref, cd_ref, ab_ref, irrep_ref, occ_ref, arrived, here,
):
    small = [
        pltpu.make_async_copy(source, target, here.at[i])
        for i, (source, target) in enumerate(
            ((cd_hbm, cd_ref), (ab_hbm, ab_ref), (irrep_hbm, irrep_ref), (occ_hbm, occ_ref))
        )
    ]
    for copy in small:
        copy.start()
    me = lax.axis_index("col")
    pairs = irrep_ref.shape[1]
    cols, cd_rows = integrals_ref.shape
    for copy in small:
        copy.wait()
    tiles = windows(cd_ref, ab_ref, me, cols, tile, cd_rows)

    def each_copy(act):
        for t, (at, size) in enumerate(tiles):
            for choice in window_sizes(cd_rows):
                @pl.when(size == choice)
                def _():
                    part = (pl.ds(t * tile, tile), pl.ds(pl.multiple_of(at, LANES), choice))
                    act(pltpu.make_async_copy(integrals_ref.at[part], packed_ref.at[part], arrived.at[t]))

    each_copy(lambda copy: copy.start())
    for t, (at, size) in enumerate(tiles):
        table_ref[2 * t] = at
        table_ref[2 * t + 1] = size
    label = irrep_ref[...]
    low = jnp.zeros((1, pairs), I32)
    high = jnp.zeros((1, pairs), I32)
    start = -me * cols
    for g in range(ab_ref.shape[0]):
        end = start + ab_ref[g]
        low = jnp.where(label == g, start, low)
        high = jnp.where(label == g, end, high)
        start = end
    occ = occ_ref[...]
    for c in range(0, cols, LANES):
        width = min(LANES, cols - c)
        spread = jnp.broadcast_to(virt_ref[:, c:c + width], (LANES, width))
        virt = jnp.transpose(spread)
        at = c + lax.broadcasted_iota(I32, (width, LANES), 0)
        for p in range(0, pairs, LANES):
            lanes = slice(p, p + LANES)
            keep = (at >= low[:, lanes]) & (at < high[:, lanes])
            weight_ref[c:c + width, lanes] = jnp.where(keep, 1.0 / (virt - occ[:, lanes]), 0.0)
    source = lax.broadcasted_iota(I32, (1, pairs), 1)
    block = source // rows
    owner = jnp.full((1, pairs), me, I32)
    for step, key in enumerate(generators(count)):
        owner = owner ^ jnp.where((block >> step) & 1 == 1, key, 0)
    place = owner * rows + (source - block * rows)
    mine = lax.broadcasted_iota(I32, (pairs, pairs), 0)
    order_ref[...] = jnp.where(mine == place, 1.0, 0.0).astype(order_ref.dtype)
    for p in range(0, pairs, LANES):
        label_ref[p:p + LANES, :] = jnp.transpose(jnp.broadcast_to(label[:, p:p + LANES].astype(F32), (LANES, LANES)))
    each_copy(lambda copy: copy.wait())


def ladder_kernel(
    total, tile, cd_ref, ab_ref, table_ref, first_ref, second_ref, packed_ref, weight_ref, order_ref, label_ref,
    update_ref, energy_ref, tau_ref, dense_ref,
):
    me = lax.axis_index("col")
    cols, cd_rows = packed_ref.shape
    pairs = order_ref.shape[0]
    half, width = first_ref.shape
    window = tau_ref.shape[1]
    irreps = cd_ref.shape[0]
    tau_ref[:, :width] = jnp.dot(
        order_ref[:, :half], first_ref[...], preferred_element_type=F32
    ) + jnp.dot(order_ref[:, half:], second_ref[...], preferred_element_type=F32)
    dense_ref[:, :cd_rows] = jnp.zeros((pairs, cd_rows), dense_ref.dtype)
    lane = lax.broadcasted_iota(I32, (1, window), 1)

    def spread(g, starts):
        cd_start, ab_start = starts
        cd_end, ab_end = cd_start + cd_ref[g], ab_start + ab_ref[g]

        @pl.when((ab_end > 0) & (ab_start < cols))
        def _():
            shift = lax.rem(cd_start, LANES)
            base = pl.multiple_of(cd_start - shift, LANES)
            moved = pltpu.roll(tau_ref[...], shift, 1)
            valid = (lane >= shift) & (lane < shift + cd_ref[g])
            here = label_ref[:, :1] == g.astype(F32)
            old = dense_ref[:, pl.ds(base, window)]
            dense_ref[:, pl.ds(base, window)] = jnp.where(valid & here, moved, old.astype(F32)).astype(old.dtype)

        return cd_end, ab_end

    lax.fori_loop(0, irreps, spread, (jnp.int32(0), -me * cols))
    energy_ref[...] = jnp.zeros((1, pairs), F32)
    for t in range(cols // tile):
        here = pl.ds(t * tile, tile)
        at, size = pl.multiple_of(table_ref[2 * t], LANES), table_ref[2 * t + 1]
        for choice in window_sizes(cd_rows):
            @pl.when(size == choice)
            def _():
                ladder = lax.dot_general(
                    packed_ref[here, pl.ds(at, choice)],
                    dense_ref[:, pl.ds(at, choice)],
                    (((1,), (1,)), ((), ())),
                    preferred_element_type=F32,
                )
                update = ladder * weight_ref[here, :]
                update_ref[here, :] = update
                energy_ref[...] += jnp.sum(ladder * update, axis=0, keepdims=True)
    energy_ref[...] = energy_ref[...] / total


def shards(tau_packed, pair_irrep, cd_sizes, ab_sizes, integrals, occ_energy, virt_energy):
    cd_rows, cols = integrals.shape
    rows, width = tau_packed.shape
    pairs = pair_irrep.shape[0]
    count = lax.axis_size("col")
    keys = generators(count)
    tile = 320 if cols % 320 == 0 else cols
    window = ceil_lanes(width + LANES - 1)
    vmem = pl.BlockSpec(memory_space=pltpu.VMEM)
    smem = pl.BlockSpec(memory_space=pltpu.SMEM)
    anywhere = pl.BlockSpec(memory_space=pl.ANY)
    near = lambda value: pltpu.with_memory_space_constraint(value, pltpu.VMEM)

    far = lambda value: pltpu.with_memory_space_constraint(value, pltpu.HBM)

    virt_row = virt_energy.reshape(1, cols)
    held = pl.pallas_call(
        copy_kernel, out_shape=pltpu.VMEM(tau_packed.shape, tau_packed.dtype), in_specs=[vmem], out_specs=vmem,
        compiler_params=pltpu.CompilerParams(vmem_limit_bytes=1 << 20),
    )(tau_packed)
    sent = tau_packed
    for step, key in enumerate(keys[:-1]):
        got = swap(sent, key, count)
        held = sent = jnp.concatenate([held, got], axis=0)
        if step == 1:
            sent, occ_energy = lax.optimization_barrier((held, occ_energy))
            held = sent
            weight, order, label, packed, table = pl.pallas_call(
                functools.partial(setup_kernel, count, rows, tile),
                out_shape=(
                    pltpu.VMEM((cols, pairs), F32),
                    pltpu.VMEM((pairs, pairs), jnp.bfloat16),
                    pltpu.VMEM((pairs, LANES), F32),
                    pltpu.VMEM((cols, cd_rows), integrals.dtype),
                    pltpu.SMEM((2 * (cols // tile),), I32),
                ),
                in_specs=[anywhere] * 4 + [vmem, anywhere],
                out_specs=(vmem, vmem, vmem, vmem, smem),
                scratch_shapes=[
                    pltpu.SMEM(cd_sizes.shape, I32),
                    pltpu.SMEM(ab_sizes.shape, I32),
                    pltpu.VMEM((1, pairs), I32),
                    pltpu.VMEM((1, pairs), F32),
                    pltpu.SemaphoreType.DMA((cols // tile,)),
                    pltpu.SemaphoreType.DMA((4,)),
                ],
                compiler_params=pltpu.CompilerParams(vmem_limit_bytes=(2 << 20) + 32 * pairs * pairs),
                cost_estimate=pl.CostEstimate(flops=10 * cols * pairs, bytes_accessed=4 * cols * pairs, transcendentals=0),
            )(
                far(cd_sizes), far(ab_sizes), far(pair_irrep.reshape(1, pairs)), far(occ_energy.reshape(1, pairs)),
                near(virt_row), far(integrals.T),
            )
        elif step == 0:
            held, virt_row = lax.optimization_barrier((held, virt_row))
            sent = held
    sent, order = lax.optimization_barrier((sent, order))
    last = swap(sent, keys[-1], count)
    update, energy = pl.pallas_call(
        functools.partial(ladder_kernel, cols * count, tile),
        out_shape=(pltpu.VMEM((cols, pairs), F32), pltpu.VMEM((1, pairs), F32)),
        in_specs=[smem, smem, smem] + [vmem] * 6,
        out_specs=(vmem, vmem),
        scratch_shapes=[pltpu.VMEM((pairs, window), F32), pltpu.VMEM((pairs, cd_rows + window), jnp.bfloat16)],
        compiler_params=pltpu.CompilerParams(vmem_limit_bytes=(8 << 20) + 32768 * pairs),
        cost_estimate=pl.CostEstimate(
            flops=2 * cols * width * pairs, bytes_accessed=2 * cols * width + 4 * cols * pairs, transcendentals=0
        ),
    )(
        cd_sizes, ab_sizes, pltpu.with_memory_space_constraint(table, pltpu.SMEM),
        near(sent), near(last), near(packed), near(weight), near(order), near(label),
    )
    for key in keys:
        energy = energy + swap(energy, key, count)
    return update.T, energy.reshape(pairs)


def solution(mesh):
    placed = (
        P(("job", "col"), None),
        P("job"),
        P("job"),
        P("job"),
        P("job", "col"),
        P("job"),
        P(("job", "col")),
    )
    return jax.shard_map(
        shards, mesh=mesh, in_specs=placed, out_specs=(P("job", "col"), P("job")), check_vma=False
    )
```

```python
import functools
import jax
import jax.numpy as jnp
from jax import lax
from jax.experimental import pallas as pl
from jax.experimental.pallas import tpu as pltpu
from jax.sharding import PartitionSpec as P

LANES = 128
F32 = jnp.float32
I32 = jnp.int32
VMEM = pl.BlockSpec(memory_space=pltpu.VMEM)
SMEM = pl.BlockSpec(memory_space=pltpu.SMEM)
ANY = pl.BlockSpec(memory_space=pl.ANY)


def generators(count):
    bits = count.bit_length() - 1
    return [(1 << b) | 1 for b in range(bits - 1, 0, -1)] + [1]


def swap(value, key, count):
    return lax.ppermute(value, "col", [(i, i ^ key) for i in range(count)])


def near(value):
    return pltpu.with_memory_space_constraint(value, pltpu.VMEM)


def far(value):
    return pltpu.with_memory_space_constraint(value, pltpu.HBM)


def window_of(width, cd_rows):
    return min(-(-(width + LANES - 1) // LANES) * LANES, cd_rows)


def window_sizes(cd_rows, width):
    most = window_of(width, cd_rows)
    return [size for size in range(256, most, 256)] + [most]


def plan(cd_ref, ab_ref, table_ref, me, cols, tile, cd_rows, width):
    sizes = window_sizes(cd_rows, width)
    tiles = cols // tile
    irreps = cd_ref.shape[0]
    fields, extras = 3 + tiles, 3 + tiles + 4 * (irreps + 1)
    starts = [(jnp.int32(0), -me * cols)]
    for g in range(irreps):
        starts.append((starts[g][0] + cd_ref[g], starts[g][1] + ab_ref[g]))
    here = [(starts[g + 1][1] > 0) & (starts[g][1] < cols) for g in range(irreps)]
    most = jnp.int32(0)
    for g in range(irreps):
        need = lax.rem(starts[g][0], LANES) + cd_ref[g]
        most = jnp.maximum(most, jnp.where(here[g], need, 0))
    size = jnp.int32(sizes[-1])
    for choice in reversed(sizes):
        size = jnp.where(most <= choice, choice, size)
    present, extra = jnp.int32(0), jnp.int32(0)
    for g in range(irreps):
        cd_start, ab_start = starts[g]
        at = jnp.minimum(cd_start - lax.rem(cd_start, LANES), cd_rows - size)
        for j, value in enumerate((jnp.int32(g), at, cd_start - at, cd_ref[g])):
            table_ref[fields + 4 * present + j] = value
        inner = jnp.maximum(ab_start, 0)
        table_ref[extras + 2 * extra] = lax.div(inner, tile)
        table_ref[extras + 2 * extra + 1] = present
        extra = extra + jnp.where(here[g] & (lax.rem(inner, tile) > 0), 1, 0)
        present = present + jnp.where(here[g], 1, 0)
    for t in range(tiles):
        passed = jnp.int32(0)
        for g in range(irreps):
            passed = passed + jnp.where(here[g] & (starts[g + 1][1] <= t * tile), 1, 0)
        table_ref[3 + t] = passed
    table_ref[0] = size
    table_ref[1] = present
    table_ref[2] = extra


def plan_kernel(tile, cd_rows, width, cols, tau_hbm, cd_hbm, ab_hbm, own_ref, table_ref, cd_ref, ab_ref, arrived):
    copies = [
        pltpu.make_async_copy(source, target, arrived.at[i])
        for i, (source, target) in enumerate(((cd_hbm, cd_ref), (ab_hbm, ab_ref), (tau_hbm, own_ref)))
    ]
    for copy in copies:
        copy.start()
    for copy in copies:
        copy.wait()
    plan(cd_ref, ab_ref, table_ref, lax.axis_index("col"), cols, tile, cd_rows, width)


def tile_copies(tile, first, extras_at, table_ref, integrals_ref, packed_ref, extra_ref, arrived, size, act):
    fields = 3 + integrals_ref.shape[0] // tile
    count = packed_ref.shape[0] // tile

    def window(t, i):
        at = pl.multiple_of(table_ref[fields + 4 * i + 1], LANES)
        return integrals_ref.at[pl.ds(pl.multiple_of(t * tile, tile), tile), pl.ds(at, size)]

    @pl.loop(0, count)
    def _(t):
        to = packed_ref.at[pl.ds(pl.multiple_of(t * tile, tile), tile), pl.ds(0, size)]
        act(pltpu.make_async_copy(window(first + t, table_ref[3 + first + t]), to, arrived.at[t]))

    if extra_ref is not None:
        @pl.loop(0, table_ref[2])
        def _(e):
            source = window(table_ref[extras_at + 2 * e], table_ref[extras_at + 2 * e + 1])
            act(pltpu.make_async_copy(source, extra_ref.at[e, :, pl.ds(0, size)], arrived.at[count + e]))


def weight_kernel(
    tile, width, table_ref, ab_hbm, irrep_hbm, occ_hbm, virt_ref, integrals_ref,
    weight_ref, label_ref, packed_ref, ab_ref, irrep_ref, occ_ref, arrived, here,
):
    copies = [
        pltpu.make_async_copy(source, target, here.at[i])
        for i, (source, target) in enumerate(((ab_hbm, ab_ref), (irrep_hbm, irrep_ref), (occ_hbm, occ_ref)))
    ]
    for copy in copies:
        copy.start()
    cols, cd_rows = integrals_ref.shape
    pairs = weight_ref.shape[1]

    def each_copy(act):
        for size in window_sizes(cd_rows, width):
            @pl.when(table_ref[0] == size)
            def _():
                tile_copies(tile, 0, 0, table_ref, integrals_ref, packed_ref, None, arrived, size, act)

    each_copy(lambda copy: copy.start())
    for copy in copies:
        copy.wait()
    label = irrep_ref[...]
    low = jnp.zeros((1, pairs), I32)
    high = jnp.zeros((1, pairs), I32)
    start = -lax.axis_index("col") * cols
    for g in range(ab_ref.shape[0]):
        end = start + ab_ref[g]
        low = jnp.where(label == g, start, low)
        high = jnp.where(label == g, end, high)
        start = end
    occ = occ_ref[...]
    for c in range(0, cols, LANES):
        span = min(LANES, cols - c)
        virt = jnp.transpose(jnp.broadcast_to(virt_ref[:, c:c + span], (LANES, span)))
        at = c + lax.broadcasted_iota(I32, (span, LANES), 0)
        for p in range(0, pairs, LANES):
            lanes = slice(p, p + LANES)
            keep = (at >= low[:, lanes]) & (at < high[:, lanes])
            weight_ref[c:c + span, lanes] = jnp.where(keep, 1.0 / (virt - occ[:, lanes]), 0.0)
    for p in range(0, pairs, LANES):
        label_ref[p:p + LANES, :] = jnp.transpose(jnp.broadcast_to(label[:, p:p + LANES].astype(F32), (LANES, LANES)))
    each_copy(lambda copy: copy.wait())


def fetch_kernel(tile, width, table_ref, after_ref, integrals_ref, packed_ref, extra_ref, mark_ref, arrived):
    del after_ref
    cols, cd_rows = integrals_ref.shape
    first = (cols - packed_ref.shape[0]) // tile
    extras_at = 3 + cols // tile + 4 * extra_ref.shape[0]
    for size in window_sizes(cd_rows, width):
        @pl.when(table_ref[0] == size)
        def _():
            args = (tile, first, extras_at, table_ref, integrals_ref, packed_ref, extra_ref, arrived, size)
            tile_copies(*args, lambda copy: copy.start())
            tile_copies(*args, lambda copy: copy.wait())
    mark_ref[...] = jnp.zeros(mark_ref.shape, F32)


def place(count, rows, first, fields, table_ref, source_ref, label_ref, tau_ref, placed_ref):
    me = lax.axis_index("col")
    half, width = source_ref.shape
    window = tau_ref.shape[1]
    keys = generators(count)
    tau_ref[:, :width] = source_ref[...].astype(F32)
    lane = lax.broadcasted_iota(I32, (1, window), 1)
    owners = []
    for block in range(half // rows):
        mask = 0 if first else keys[-1]
        for step, key in enumerate(keys[:-1]):
            mask ^= key if (block >> step) & 1 else 0
        owners.append(me ^ mask)
    labels = jnp.concatenate(
        [label_ref[pl.ds(pl.multiple_of(owner * rows, rows), rows), :] for owner in owners], axis=0
    )[:, :1]

    def moved(i):
        place_at, size = table_ref[fields + 4 * i + 2], table_ref[fields + 4 * i + 3]
        return jnp.where((lane >= place_at) & (lane < place_at + size), pltpu.roll(tau_ref[...], place_at, 1), 0.0)

    def store(values):
        for block, owner in enumerate(owners):
            to = pl.ds(pl.multiple_of(lax.div(owner, 2) * rows, rows), rows)
            placed_ref[to, :] = values[block * rows:(block + 1) * rows]

    store(moved(0))

    @pl.loop(1, table_ref[1])
    def _(i):
        old = jnp.concatenate(
            [placed_ref[pl.ds(pl.multiple_of(lax.div(owner, 2) * rows, rows), rows), :] for owner in owners], axis=0
        )
        store(jnp.where(labels == table_ref[fields + 4 * i].astype(F32), moved(i), old))


def first_kernel(count, rows, fields, table_ref, source_ref, label_ref, after_ref, placed_ref, tau_ref):
    del after_ref
    place(count, rows, True, fields, table_ref, source_ref, label_ref, tau_ref, placed_ref)


def ladder_kernel(
    count, rows, total, tile, width, cd_rows, table_ref, second_ref, label_ref, first_ref, early_ref, packed_ref, extra_ref, weight_ref,
    update_ref, energy_ref, tau_ref, other_ref, dense_ref, parts_ref,
):
    cols, pairs = weight_ref.shape
    half, window = tau_ref.shape
    tiles = cols // tile
    fields, extras = 3 + tiles, 3 + tiles + 4 * extra_ref.shape[0]
    place(count, rows, False, fields, table_ref, second_ref, label_ref, tau_ref, other_ref)
    me = lax.axis_index("col")

    def in_order(chip):
        flips = lax.shift_right_logical(me, 1) ^ chip
        odd = me & 1
        for step in range(len(generators(count)) - 1):
            odd = odd ^ (lax.shift_right_logical(flips, step) & 1)
        here = slice(chip * rows, (chip + 1) * rows)
        own, other = first_ref[here], other_ref[here]
        return [jnp.where(odd == 1, other, own), jnp.where(odd == 1, own, other)]

    @pl.loop(0, table_ref[1])
    def _(i):
        both = jnp.concatenate([part for chip in range(half // rows) for part in in_order(chip)], axis=0)
        mine = label_ref[:, :1] == table_ref[fields + 4 * i].astype(F32)
        dense_ref[i] = jnp.where(mine, both, 0.0).astype(dense_ref.dtype)

    def integrals_of(t, size):
        early = early_ref.shape[0] // tile
        source, t = (early_ref, t) if t < early else (packed_ref, t - early)
        return source[t * tile:(t + 1) * tile, :size]

    def ladder_tile(integrals, i, here, size):
        ladder = lax.dot_general(
            integrals, dense_ref[i, :, :size], (((1,), (1,)), ((), ())), preferred_element_type=F32
        )
        update = ladder * weight_ref[here, :]
        return update, jnp.sum((ladder * update).reshape(tile // 8, 8, pairs), axis=0)

    for size in window_sizes(cd_rows, width):
        @pl.when(table_ref[0] == size)
        def _():
            for t in range(tiles):
                here = pl.ds(t * tile, tile)
                update_ref[here, :], parts_ref[t] = ladder_tile(integrals_of(t, size), table_ref[3 + t], here, size)

            @pl.loop(0, table_ref[2])
            def _(e):
                t, i = table_ref[extras + 2 * e], table_ref[extras + 2 * e + 1]
                here = pl.ds(pl.multiple_of(t * tile, tile), tile)
                update, part = ladder_tile(extra_ref[e, :, :size], i, here, size)
                update_ref[here, :] += update
                parts_ref[t] += part

    energy_ref[...] = jnp.sum(jnp.sum(parts_ref[...], axis=0), axis=0, keepdims=True) / total


def shards(tau_packed, pair_irrep, cd_sizes, ab_sizes, integrals, occ_energy, virt_energy):
    cd_rows, cols = integrals.shape
    rows, width = tau_packed.shape
    pairs = pair_irrep.shape[0]
    irreps = cd_sizes.shape[0]
    count = lax.axis_size("col")
    keys = generators(count)
    tile = 160 if cols % 160 == 0 else cols
    tiles = cols // tile
    fields = 3 + tiles
    window = window_of(width, cd_rows)
    entries = fields + 4 * (irreps + 1) + 2 * (irreps + 1)

    early = (tiles * 6 // 10) * tile
    virt_row = virt_energy.reshape(1, cols)
    turned = far(integrals.T)
    held, table = pl.pallas_call(
        functools.partial(plan_kernel, tile, cd_rows, width, cols),
        out_shape=(pltpu.VMEM(tau_packed.shape, tau_packed.dtype), pltpu.SMEM((entries,), I32)),
        in_specs=[ANY] * 3,
        out_specs=(VMEM, SMEM),
        scratch_shapes=[
            pltpu.SMEM(cd_sizes.shape, I32), pltpu.SMEM(ab_sizes.shape, I32), pltpu.SemaphoreType.DMA((3,)),
        ],
        compiler_params=pltpu.CompilerParams(vmem_limit_bytes=1 << 20),
        cost_estimate=pl.CostEstimate(flops=0, bytes_accessed=1 << 20, transcendentals=0),
    )(far(tau_packed), far(cd_sizes), far(ab_sizes))
    table = pltpu.with_memory_space_constraint(table, pltpu.SMEM)
    sent = tau_packed
    for step, key in enumerate(keys[:-1]):
        held = jnp.concatenate([held, swap(sent, key, count)], axis=0)
        if step == 0:
            held, virt_row, occ_energy = lax.optimization_barrier((held, virt_row, occ_energy))
            weight, label, packed_early = pl.pallas_call(
                functools.partial(weight_kernel, tile, width),
                out_shape=(
                    pltpu.VMEM((cols, pairs), F32),
                    pltpu.VMEM((pairs, LANES), F32),
                    pltpu.VMEM((early, window), integrals.dtype),
                ),
                in_specs=[SMEM] + [ANY] * 3 + [VMEM, ANY],
                out_specs=(VMEM, VMEM, VMEM),
                scratch_shapes=[
                    pltpu.SMEM(ab_sizes.shape, I32),
                    pltpu.VMEM((1, pairs), I32),
                    pltpu.VMEM((1, pairs), F32),
                    pltpu.SemaphoreType.DMA((tiles,)),
                    pltpu.SemaphoreType.DMA((3,)),
                ],
                compiler_params=pltpu.CompilerParams(vmem_limit_bytes=2 << 20),
                cost_estimate=pl.CostEstimate(flops=10 * cols * pairs, bytes_accessed=4 * cols * pairs, transcendentals=0),
            )(
                table, far(ab_sizes), far(pair_irrep.reshape(1, pairs)), far(occ_energy.reshape(1, pairs)),
                near(virt_row), turned,
            )
        elif step == 1:
            held, label = lax.optimization_barrier((held, label))
            packed, extra, mark = pl.pallas_call(
                functools.partial(fetch_kernel, tile, width),
                out_shape=(
                    pltpu.VMEM((cols - early, window), integrals.dtype),
                    pltpu.VMEM((irreps + 1, tile, window), integrals.dtype),
                    pltpu.VMEM((8, LANES), F32),
                ),
                in_specs=[SMEM, ANY, ANY],
                out_specs=(VMEM, VMEM, VMEM),
                scratch_shapes=[pltpu.SemaphoreType.DMA((tiles + irreps + 1,))],
                compiler_params=pltpu.CompilerParams(vmem_limit_bytes=1 << 20),
                cost_estimate=pl.CostEstimate(flops=0, bytes_accessed=2 * cols * width, transcendentals=0),
            )(table, near(label), turned)
        elif step == 2:
            held, mark = lax.optimization_barrier((held, mark))
        else:
            held = lax.optimization_barrier(held)
        sent = held
    second = swap(held, keys[-1], count)
    first = pl.pallas_call(
        functools.partial(first_kernel, count, rows, fields),
        out_shape=pltpu.VMEM((pairs // 2, window), F32),
        in_specs=[SMEM, VMEM, VMEM, ANY],
        out_specs=VMEM,
        scratch_shapes=[pltpu.VMEM((pairs // 2, window), F32)],
        compiler_params=pltpu.CompilerParams(vmem_limit_bytes=(1 << 20) + 16 * pairs * window),
        cost_estimate=pl.CostEstimate(flops=10 * pairs * window, bytes_accessed=4 * pairs * window, transcendentals=0),
    )(table, near(held), near(label), near(mark))
    update, energy = pl.pallas_call(
        functools.partial(ladder_kernel, count, rows, cols * count, tile, width, cd_rows),
        out_shape=(pltpu.VMEM((cols, pairs), F32), pltpu.VMEM((1, pairs), F32)),
        in_specs=[SMEM] + [VMEM] * 7,
        out_specs=(VMEM, VMEM),
        scratch_shapes=[
            pltpu.VMEM((pairs // 2, window), F32),
            pltpu.VMEM((pairs // 2, window), F32),
            pltpu.VMEM((irreps, pairs, window), jnp.bfloat16),
            pltpu.VMEM((tiles, 8, pairs), F32),
        ],
        compiler_params=pltpu.CompilerParams(vmem_limit_bytes=(4 << 20) + 32 * pairs * window),
        cost_estimate=pl.CostEstimate(
            flops=2 * cols * width * pairs, bytes_accessed=2 * cols * width + 4 * cols * pairs, transcendentals=0
        ),
    )(table, near(second), near(label), near(first), near(packed_early), near(packed), near(extra), near(weight))
    for key in keys:
        energy = energy + swap(energy, key, count)
    return update.T, energy.reshape(pairs)


def solution(mesh):
    placed = (
        P(("job", "col"), None),
        P("job"),
        P("job"),
        P("job"),
        P("job", "col"),
        P("job"),
        P(("job", "col")),
    )
    return jax.shard_map(
        shards, mesh=mesh, in_specs=placed, out_specs=(P("job", "col"), P("job")), check_vma=False
    )
```

```python
import functools
import jax
import jax.numpy as jnp
from jax import lax
from jax.experimental import pallas as pl
from jax.experimental.pallas import tpu as pltpu
from jax.sharding import PartitionSpec as P

LANES = 128
F32 = jnp.float32
I32 = jnp.int32
VMEM = pl.BlockSpec(memory_space=pltpu.VMEM)
SMEM = pl.BlockSpec(memory_space=pltpu.SMEM)
ANY = pl.BlockSpec(memory_space=pl.ANY)


def generators(count):
    bits = count.bit_length() - 1
    return [(1 << b) | 1 for b in range(bits - 1, 0, -1)] + [1]


def swap(value, key, count):
    return lax.ppermute(value, "col", [(i, i ^ key) for i in range(count)])


def near(value):
    return pltpu.with_memory_space_constraint(value, pltpu.VMEM)


def far(value):
    return pltpu.with_memory_space_constraint(value, pltpu.HBM)


def window_of(width, cd_rows):
    return min(-(-(width + LANES - 1) // LANES) * LANES, cd_rows)


def window_sizes(cd_rows, width):
    most = window_of(width, cd_rows)
    return [size for size in range(256, most, 256)] + [most]


def fields_of(tiles, irreps):
    return 3 + 2 * tiles, 3 + 2 * tiles + 4 * (irreps + 1)


def plan(cd_ref, ab_ref, table_ref, me, cols, tile, cd_rows, width):
    sizes = window_sizes(cd_rows, width)
    tiles = cols // tile
    irreps = cd_ref.shape[0]
    fields, extras = fields_of(tiles, irreps)
    starts = [(jnp.int32(0), -me * cols)]
    for g in range(irreps):
        starts.append((starts[g][0] + cd_ref[g], starts[g][1] + ab_ref[g]))
    here = [(starts[g + 1][1] > 0) & (starts[g][1] < cols) for g in range(irreps)]
    most = jnp.int32(0)
    for g in range(irreps):
        need = lax.rem(starts[g][0], LANES) + cd_ref[g]
        most = jnp.maximum(most, jnp.where(here[g], need, 0))
    size = jnp.int32(sizes[-1])
    for choice in reversed(sizes):
        size = jnp.where(most <= choice, choice, size)
    present, extra = jnp.int32(0), jnp.int32(0)
    for g in range(irreps):
        cd_start, ab_start = starts[g]
        at = jnp.minimum(cd_start - lax.rem(cd_start, LANES), cd_rows - size)
        for j, value in enumerate((jnp.int32(g), at, cd_start - at, cd_ref[g])):
            table_ref[fields + 4 * present + j] = value
        inner = jnp.maximum(ab_start, 0)
        t = lax.div(inner, tile)
        for j, value in enumerate((t, present, inner - t * tile, starts[g + 1][1] - t * tile)):
            table_ref[extras + 4 * extra + j] = value
        extra = extra + jnp.where(here[g] & (lax.rem(inner, tile) > 0), 1, 0)
        present = present + jnp.where(here[g], 1, 0)
    for t in range(tiles):
        passed = jnp.int32(0)
        for g in range(irreps):
            passed = passed + jnp.where(here[g] & (starts[g + 1][1] <= t * tile), 1, 0)
        end = jnp.int32(tile)
        for g in reversed(range(irreps)):
            end = jnp.where(starts[g + 1][1] > t * tile, starts[g + 1][1] - t * tile, end)
        table_ref[3 + 2 * t] = passed
        table_ref[4 + 2 * t] = end
    for j in range(4):
        table_ref[extras + 4 * extra + j] = jnp.int32(0)
    table_ref[0] = size
    table_ref[1] = present
    table_ref[2] = extra


def plan_kernel(tile, cd_rows, width, cols, tau_hbm, cd_hbm, ab_hbm, own_ref, table_ref, cd_ref, ab_ref, arrived):
    copies = [
        pltpu.make_async_copy(source, target, arrived.at[i])
        for i, (source, target) in enumerate(((cd_hbm, cd_ref), (ab_hbm, ab_ref), (tau_hbm, own_ref)))
    ]
    for copy in copies:
        copy.start()
    for copy in copies:
        copy.wait()
    plan(cd_ref, ab_ref, table_ref, lax.axis_index("col"), cols, tile, cd_rows, width)


def tile_copies(tile, first, extras_at, table_ref, integrals_ref, packed_ref, extra_ref, arrived, size, act):
    fields, _ = fields_of(integrals_ref.shape[0] // tile, 0)
    count = packed_ref.shape[0] // tile

    def window(t, i):
        at = pl.multiple_of(table_ref[fields + 4 * i + 1], LANES)
        return integrals_ref.at[pl.ds(pl.multiple_of(t * tile, tile), tile), pl.ds(at, size)]

    @pl.loop(0, count)
    def _(t):
        to = packed_ref.at[pl.ds(pl.multiple_of(t * tile, tile), tile), pl.ds(0, size)]
        act(pltpu.make_async_copy(window(first + t, table_ref[3 + 2 * (first + t)]), to, arrived.at[t]))

    if extra_ref is not None:
        @pl.loop(0, table_ref[2])
        def _(e):
            source = window(table_ref[extras_at + 4 * e], table_ref[extras_at + 4 * e + 1])
            act(pltpu.make_async_copy(source, extra_ref.at[e, :, pl.ds(0, size)], arrived.at[count + e]))


def weight_kernel(
    tile, width, table_ref, ab_hbm, irrep_hbm, occ_hbm, virt_ref, integrals_ref,
    weight_ref, label_ref, packed_ref, ab_ref, irrep_ref, occ_ref, arrived, here,
):
    copies = [
        pltpu.make_async_copy(source, target, here.at[i])
        for i, (source, target) in enumerate(((ab_hbm, ab_ref), (irrep_hbm, irrep_ref), (occ_hbm, occ_ref)))
    ]
    for copy in copies:
        copy.start()
    cols, cd_rows = integrals_ref.shape
    pairs = weight_ref.shape[1]

    def each_copy(act):
        for size in window_sizes(cd_rows, width):
            @pl.when(table_ref[0] == size)
            def _():
                tile_copies(tile, 0, 0, table_ref, integrals_ref, packed_ref, None, arrived, size, act)

    each_copy(lambda copy: copy.start())
    for copy in copies:
        copy.wait()
    label = irrep_ref[...]
    low = jnp.zeros((1, pairs), I32)
    high = jnp.zeros((1, pairs), I32)
    start = -lax.axis_index("col") * cols
    for g in range(ab_ref.shape[0]):
        end = start + ab_ref[g]
        low = jnp.where(label == g, start, low)
        high = jnp.where(label == g, end, high)
        start = end
    occ = occ_ref[...]
    for c in range(0, cols, LANES):
        span = min(LANES, cols - c)
        virt = jnp.transpose(jnp.broadcast_to(virt_ref[:, c:c + span], (LANES, span)))
        at = c + lax.broadcasted_iota(I32, (span, LANES), 0)
        for p in range(0, pairs, LANES):
            lanes = slice(p, p + LANES)
            keep = (at >= low[:, lanes]) & (at < high[:, lanes])
            weight_ref[c:c + span, lanes] = jnp.where(keep, 1.0 / (virt - occ[:, lanes]), 0.0)
    for p in range(0, pairs, LANES):
        label_ref[p:p + LANES, :] = jnp.transpose(jnp.broadcast_to(label[:, p:p + LANES].astype(F32), (LANES, LANES)))
    each_copy(lambda copy: copy.wait())


def fetch_kernel(tile, width, table_ref, after_ref, integrals_ref, packed_ref, extra_ref, mark_ref, arrived):
    del after_ref
    cols, cd_rows = integrals_ref.shape
    first = (cols - packed_ref.shape[0]) // tile
    _, extras_at = fields_of(cols // tile, extra_ref.shape[0] - 1)
    for size in window_sizes(cd_rows, width):
        @pl.when(table_ref[0] == size)
        def _():
            args = (tile, first, extras_at, table_ref, integrals_ref, packed_ref, extra_ref, arrived, size)
            tile_copies(*args, lambda copy: copy.start())
            tile_copies(*args, lambda copy: copy.wait())
    mark_ref[...] = jnp.zeros(mark_ref.shape, F32)


def place(count, rows, first, fields, table_ref, source_ref, label_ref, tau_ref, placed_ref):
    me = lax.axis_index("col")
    half, width = source_ref.shape
    window = tau_ref.shape[1]
    keys = generators(count)
    tau_ref[:, :width] = source_ref[...].astype(F32)
    lane = lax.broadcasted_iota(I32, (1, window), 1)
    owners = []
    for block in range(half // rows):
        mask = 0 if first else keys[-1]
        for step, key in enumerate(keys[:-1]):
            mask ^= key if (block >> step) & 1 else 0
        owners.append(me ^ mask)
    labels = jnp.concatenate(
        [label_ref[pl.ds(pl.multiple_of(owner * rows, rows), rows), :] for owner in owners], axis=0
    )[:, :1]

    def moved(i):
        place_at, size = table_ref[fields + 4 * i + 2], table_ref[fields + 4 * i + 3]
        return jnp.where((lane >= place_at) & (lane < place_at + size), pltpu.roll(tau_ref[...], place_at, 1), 0.0)

    def store(values):
        for block, owner in enumerate(owners):
            to = pl.ds(pl.multiple_of(lax.div(owner, 2) * rows, rows), rows)
            placed_ref[to, :] = values[block * rows:(block + 1) * rows]

    store(moved(0))

    @pl.loop(1, table_ref[1])
    def _(i):
        old = jnp.concatenate(
            [placed_ref[pl.ds(pl.multiple_of(lax.div(owner, 2) * rows, rows), rows), :] for owner in owners], axis=0
        )
        store(jnp.where(labels == table_ref[fields + 4 * i].astype(F32), moved(i), old))


def first_kernel(count, rows, fields, table_ref, source_ref, label_ref, after_ref, placed_ref, tau_ref):
    del after_ref
    place(count, rows, True, fields, table_ref, source_ref, label_ref, tau_ref, placed_ref)


def ladder_kernel(
    count, rows, total, tile, width, cd_rows, table_ref, second_ref, label_ref, first_ref, early_ref, packed_ref, extra_ref, weight_ref,
    update_ref, energy_ref, tau_ref, other_ref, dense_ref, parts_ref,
):
    cols, pairs = weight_ref.shape
    half, window = tau_ref.shape
    tiles = cols // tile
    fields, extras = fields_of(tiles, extra_ref.shape[0] - 1)
    place(count, rows, False, fields, table_ref, second_ref, label_ref, tau_ref, other_ref)
    me = lax.axis_index("col")

    def in_order(chip):
        flips = lax.shift_right_logical(me, 1) ^ chip
        odd = me & 1
        for step in range(len(generators(count)) - 1):
            odd = odd ^ (lax.shift_right_logical(flips, step) & 1)
        here = slice(chip * rows, (chip + 1) * rows)
        own, other = first_ref[here], other_ref[here]
        return [jnp.where(odd == 1, other, own), jnp.where(odd == 1, own, other)]

    both = jnp.concatenate([part for chip in range(half // rows) for part in in_order(chip)], axis=0)
    dense_ref[...] = both.astype(dense_ref.dtype)

    def integrals_of(t, size):
        early = early_ref.shape[0] // tile
        source, t = (early_ref, t) if t < early else (packed_ref, t - early)
        return source[t * tile:(t + 1) * tile, :size]

    row = lax.broadcasted_iota(I32, (tile, LANES), 0)
    row = jnp.concatenate([row] * (pairs // LANES), axis=1)

    def ladder_tile(integrals, begin, end, here, size):
        ladder = lax.dot_general(
            integrals, dense_ref[:, :size], (((1,), (1,)), ((), ())), preferred_element_type=F32
        )
        ladder = jnp.where((row >= begin) & (row < end) if begin is not None else row < end, ladder, 0.0)
        update = ladder * weight_ref[here, :]
        return update, jnp.sum((ladder * update).reshape(tile // 8, 8, pairs), axis=0)

    def extra_job(e, size):
        t, begin, end = (table_ref[extras + 4 * e + j] for j in (0, 2, 3))
        here = pl.ds(pl.multiple_of(t * tile, tile), tile)
        update, part = ladder_tile(extra_ref[e, :, :size], begin, end, here, size)
        update_ref[here, :] += update
        parts_ref[tiles + e] = part

    parts_ref[tiles + 1:] = jnp.zeros((parts_ref.shape[0] - tiles - 1,) + parts_ref.shape[1:], F32)
    for size in window_sizes(cd_rows, width):
        @pl.when(table_ref[0] == size)
        def _():
            for t in range(tiles):
                here = pl.ds(t * tile, tile)
                update_ref[here, :], parts_ref[t] = ladder_tile(
                    integrals_of(t, size), None, table_ref[4 + 2 * t], here, size
                )
            extra_job(0, size)

            @pl.loop(1, table_ref[2])
            def _(e):
                extra_job(e, size)

    energy_ref[...] = jnp.sum(jnp.sum(parts_ref[...], axis=0), axis=0, keepdims=True) / total


def shards(tau_packed, pair_irrep, cd_sizes, ab_sizes, integrals, occ_energy, virt_energy):
    cd_rows, cols = integrals.shape
    rows, width = tau_packed.shape
    pairs = pair_irrep.shape[0]
    irreps = cd_sizes.shape[0]
    count = lax.axis_size("col")
    keys = generators(count)
    tile = 160 if cols % 160 == 0 else cols
    tiles = cols // tile
    fields, extras = fields_of(tiles, irreps)
    window = window_of(width, cd_rows)
    entries = extras + 4 * (irreps + 1)

    early = (tiles * 6 // 10) * tile
    virt_row = virt_energy.reshape(1, cols)
    turned = far(integrals.T)
    held, table = pl.pallas_call(
        functools.partial(plan_kernel, tile, cd_rows, width, cols),
        out_shape=(pltpu.VMEM(tau_packed.shape, tau_packed.dtype), pltpu.SMEM((entries,), I32)),
        in_specs=[ANY] * 3,
        out_specs=(VMEM, SMEM),
        scratch_shapes=[
            pltpu.SMEM(cd_sizes.shape, I32), pltpu.SMEM(ab_sizes.shape, I32), pltpu.SemaphoreType.DMA((3,)),
        ],
        compiler_params=pltpu.CompilerParams(vmem_limit_bytes=1 << 20),
        cost_estimate=pl.CostEstimate(flops=0, bytes_accessed=1 << 20, transcendentals=0),
    )(far(tau_packed), far(cd_sizes), far(ab_sizes))
    table = pltpu.with_memory_space_constraint(table, pltpu.SMEM)
    sent = tau_packed
    for step, key in enumerate(keys[:-1]):
        held = jnp.concatenate([held, swap(sent, key, count)], axis=0)
        if step == 0:
            held, virt_row, occ_energy = lax.optimization_barrier((held, virt_row, occ_energy))
            weight, label, packed_early = pl.pallas_call(
                functools.partial(weight_kernel, tile, width),
                out_shape=(
                    pltpu.VMEM((cols, pairs), F32),
                    pltpu.VMEM((pairs, LANES), F32),
                    pltpu.VMEM((early, window), integrals.dtype),
                ),
                in_specs=[SMEM] + [ANY] * 3 + [VMEM, ANY],
                out_specs=(VMEM, VMEM, VMEM),
                scratch_shapes=[
                    pltpu.SMEM(ab_sizes.shape, I32),
                    pltpu.VMEM((1, pairs), I32),
                    pltpu.VMEM((1, pairs), F32),
                    pltpu.SemaphoreType.DMA((tiles,)),
                    pltpu.SemaphoreType.DMA((3,)),
                ],
                compiler_params=pltpu.CompilerParams(vmem_limit_bytes=2 << 20),
                cost_estimate=pl.CostEstimate(flops=10 * cols * pairs, bytes_accessed=4 * cols * pairs, transcendentals=0),
            )(
                table, far(ab_sizes), far(pair_irrep.reshape(1, pairs)), far(occ_energy.reshape(1, pairs)),
                near(virt_row), turned,
            )
        elif step == 1:
            held, label = lax.optimization_barrier((held, label))
            packed, extra, mark = pl.pallas_call(
                functools.partial(fetch_kernel, tile, width),
                out_shape=(
                    pltpu.VMEM((cols - early, window), integrals.dtype),
                    pltpu.VMEM((irreps + 1, tile, window), integrals.dtype),
                    pltpu.VMEM((8, LANES), F32),
                ),
                in_specs=[SMEM, ANY, ANY],
                out_specs=(VMEM, VMEM, VMEM),
                scratch_shapes=[pltpu.SemaphoreType.DMA((tiles + irreps + 1,))],
                compiler_params=pltpu.CompilerParams(vmem_limit_bytes=1 << 20),
                cost_estimate=pl.CostEstimate(flops=0, bytes_accessed=2 * cols * width, transcendentals=0),
            )(table, near(label), turned)
        elif step == 2:
            held, mark = lax.optimization_barrier((held, mark))
        else:
            held = lax.optimization_barrier(held)
        sent = held
    second = swap(held, keys[-1], count)
    first = pl.pallas_call(
        functools.partial(first_kernel, count, rows, fields),
        out_shape=pltpu.VMEM((pairs // 2, window), F32),
        in_specs=[SMEM, VMEM, VMEM, ANY],
        out_specs=VMEM,
        scratch_shapes=[pltpu.VMEM((pairs // 2, window), F32)],
        compiler_params=pltpu.CompilerParams(vmem_limit_bytes=(1 << 20) + 16 * pairs * window),
        cost_estimate=pl.CostEstimate(flops=10 * pairs * window, bytes_accessed=4 * pairs * window, transcendentals=0),
    )(table, near(held), near(label), near(mark))
    update, energy = pl.pallas_call(
        functools.partial(ladder_kernel, count, rows, cols * count, tile, width, cd_rows),
        out_shape=(pltpu.VMEM((cols, pairs), F32), pltpu.VMEM((1, pairs), F32)),
        in_specs=[SMEM] + [VMEM] * 7,
        out_specs=(VMEM, VMEM),
        scratch_shapes=[
            pltpu.VMEM((pairs // 2, window), F32),
            pltpu.VMEM((pairs // 2, window), F32),
            pltpu.VMEM((pairs, window), jnp.bfloat16),
            pltpu.VMEM((tiles + irreps + 1, 8, pairs), F32),
        ],
        compiler_params=pltpu.CompilerParams(vmem_limit_bytes=(4 << 20) + 32 * pairs * window),
        cost_estimate=pl.CostEstimate(
            flops=2 * cols * width * pairs, bytes_accessed=2 * cols * width + 4 * cols * pairs, transcendentals=0
        ),
    )(table, near(second), near(label), near(first), near(packed_early), near(packed), near(extra), near(weight))
    for key in keys:
        energy = energy + swap(energy, key, count)
    return update.T, energy.reshape(pairs)


def solution(mesh):
    placed = (
        P(("job", "col"), None),
        P("job"),
        P("job"),
        P("job"),
        P("job", "col"),
        P("job"),
        P(("job", "col")),
    )
    return jax.shard_map(
        shards, mesh=mesh, in_specs=placed, out_specs=(P("job", "col"), P("job")), check_vma=False
    )
```

```python
import functools
import jax
import jax.numpy as jnp
from jax import lax
from jax.experimental import pallas as pl
from jax.experimental.pallas import tpu as pltpu
from jax.sharding import PartitionSpec as P

LANES = 128
F32 = jnp.float32
I32 = jnp.int32
VMEM = pl.BlockSpec(memory_space=pltpu.VMEM)
SMEM = pl.BlockSpec(memory_space=pltpu.SMEM)
ANY = pl.BlockSpec(memory_space=pl.ANY)


def generators(count):
    bits = count.bit_length() - 1
    return [(1 << b) | 1 for b in range(bits - 1, 0, -1)] + [1]


def swap(value, key, count):
    return lax.ppermute(value, "col", [(i, i ^ key) for i in range(count)])


def near(value):
    return pltpu.with_memory_space_constraint(value, pltpu.VMEM)


def far(value):
    return pltpu.with_memory_space_constraint(value, pltpu.HBM)


def window_of(width, cd_rows):
    return min(-(-(width + LANES - 1) // LANES) * LANES, cd_rows)


def window_sizes(cd_rows, width):
    most = window_of(width, cd_rows)
    return [size for size in range(256, most, 256)] + [most]


def fields_of(tiles, irreps):
    return 3 + 2 * tiles, 3 + 2 * tiles + 4 * (irreps + 1)


def plan(cd_ref, ab_ref, table_ref, me, cols, tile, cd_rows, width):
    sizes = window_sizes(cd_rows, width)
    tiles = cols // tile
    irreps = cd_ref.shape[0]
    fields, extras = fields_of(tiles, irreps)
    starts = [(jnp.int32(0), -me * cols)]
    for g in range(irreps):
        starts.append((starts[g][0] + cd_ref[g], starts[g][1] + ab_ref[g]))
    here = [(starts[g + 1][1] > 0) & (starts[g][1] < cols) for g in range(irreps)]
    most = jnp.int32(0)
    for g in range(irreps):
        need = lax.rem(starts[g][0], LANES) + cd_ref[g]
        most = jnp.maximum(most, jnp.where(here[g], need, 0))
    size = jnp.int32(sizes[-1])
    for choice in reversed(sizes):
        size = jnp.where(most <= choice, choice, size)
    present, extra = jnp.int32(0), jnp.int32(0)
    for g in range(irreps):
        cd_start, ab_start = starts[g]
        at = jnp.minimum(cd_start - lax.rem(cd_start, LANES), cd_rows - size)
        for j, value in enumerate((jnp.int32(g), at, cd_start - at, cd_ref[g])):
            table_ref[fields + 4 * present + j] = value
        inner = jnp.maximum(ab_start, 0)
        t = lax.div(inner, tile)
        for j, value in enumerate((t, present, inner - t * tile, starts[g + 1][1] - t * tile)):
            table_ref[extras + 4 * extra + j] = value
        extra = extra + jnp.where(here[g] & (lax.rem(inner, tile) > 0), 1, 0)
        present = present + jnp.where(here[g], 1, 0)
    for t in range(tiles):
        passed = jnp.int32(0)
        for g in range(irreps):
            passed = passed + jnp.where(here[g] & (starts[g + 1][1] <= t * tile), 1, 0)
        end = jnp.int32(tile)
        for g in reversed(range(irreps)):
            end = jnp.where(starts[g + 1][1] > t * tile, starts[g + 1][1] - t * tile, end)
        table_ref[3 + 2 * t] = passed
        table_ref[4 + 2 * t] = end
    for j in range(4):
        table_ref[extras + 4 * extra + j] = jnp.int32(0)
    table_ref[0] = size
    table_ref[1] = present
    table_ref[2] = extra


def plan_kernel(tile, cd_rows, width, cols, tau_hbm, cd_hbm, ab_hbm, own_ref, table_ref, cd_ref, ab_ref, arrived):
    copies = [
        pltpu.make_async_copy(source, target, arrived.at[i])
        for i, (source, target) in enumerate(((cd_hbm, cd_ref), (ab_hbm, ab_ref), (tau_hbm, own_ref)))
    ]
    for copy in copies:
        copy.start()
    for copy in copies:
        copy.wait()
    plan(cd_ref, ab_ref, table_ref, lax.axis_index("col"), cols, tile, cd_rows, width)


def tile_copies(tile, first, extras_at, table_ref, integrals_ref, packed_ref, extra_ref, arrived, size, act):
    fields, _ = fields_of(integrals_ref.shape[0] // tile, 0)
    count = packed_ref.shape[0] // tile

    def window(t, i):
        at = pl.multiple_of(table_ref[fields + 4 * i + 1], LANES)
        return integrals_ref.at[pl.ds(pl.multiple_of(t * tile, tile), tile), pl.ds(at, size)]

    @pl.loop(0, count)
    def _(t):
        to = packed_ref.at[pl.ds(pl.multiple_of(t * tile, tile), tile), pl.ds(0, size)]
        act(pltpu.make_async_copy(window(first + t, table_ref[3 + 2 * (first + t)]), to, arrived.at[t]))

    if extra_ref is not None:
        @pl.loop(0, table_ref[2])
        def _(e):
            source = window(table_ref[extras_at + 4 * e], table_ref[extras_at + 4 * e + 1])
            act(pltpu.make_async_copy(source, extra_ref.at[e, :, pl.ds(0, size)], arrived.at[count + e]))


def weight_kernel(
    tile, width, table_ref, ab_hbm, irrep_hbm, occ_hbm, virt_ref, integrals_ref,
    weight_ref, label_ref, packed_ref, ab_ref, irrep_ref, occ_ref, arrived, here,
):
    copies = [
        pltpu.make_async_copy(source, target, here.at[i])
        for i, (source, target) in enumerate(((ab_hbm, ab_ref), (irrep_hbm, irrep_ref), (occ_hbm, occ_ref)))
    ]
    for copy in copies:
        copy.start()
    cols, cd_rows = integrals_ref.shape
    pairs = weight_ref.shape[1]

    def each_copy(act):
        for size in window_sizes(cd_rows, width):
            @pl.when(table_ref[0] == size)
            def _():
                tile_copies(tile, 0, 0, table_ref, integrals_ref, packed_ref, None, arrived, size, act)

    each_copy(lambda copy: copy.start())
    for copy in copies:
        copy.wait()
    label = irrep_ref[...]
    low = jnp.zeros((1, pairs), I32)
    high = jnp.zeros((1, pairs), I32)
    start = -lax.axis_index("col") * cols
    for g in range(ab_ref.shape[0]):
        end = start + ab_ref[g]
        low = jnp.where(label == g, start, low)
        high = jnp.where(label == g, end, high)
        start = end
    occ = occ_ref[...]
    for c in range(0, cols, LANES):
        span = min(LANES, cols - c)
        virt = jnp.transpose(jnp.broadcast_to(virt_ref[:, c:c + span], (LANES, span)))
        at = c + lax.broadcasted_iota(I32, (span, LANES), 0)
        for p in range(0, pairs, LANES):
            lanes = slice(p, p + LANES)
            keep = (at >= low[:, lanes]) & (at < high[:, lanes])
            weight_ref[c:c + span, lanes] = jnp.where(keep, 1.0 / (virt - occ[:, lanes]), 0.0)
    for p in range(0, pairs, LANES):
        label_ref[p:p + LANES, :] = jnp.transpose(jnp.broadcast_to(label[:, p:p + LANES].astype(F32), (LANES, LANES)))
    each_copy(lambda copy: copy.wait())


def fetch_kernel(tile, width, table_ref, after_ref, integrals_ref, packed_ref, extra_ref, mark_ref, arrived):
    del after_ref
    cols, cd_rows = integrals_ref.shape
    first = (cols - packed_ref.shape[0]) // tile
    _, extras_at = fields_of(cols // tile, extra_ref.shape[0] - 1)
    for size in window_sizes(cd_rows, width):
        @pl.when(table_ref[0] == size)
        def _():
            args = (tile, first, extras_at, table_ref, integrals_ref, packed_ref, extra_ref, arrived, size)
            tile_copies(*args, lambda copy: copy.start())
            tile_copies(*args, lambda copy: copy.wait())
    mark_ref[...] = jnp.zeros(mark_ref.shape, F32)


def place(count, rows, mask, fields, table_ref, source, label_ref, tau_ref, placed_ref):
    me = lax.axis_index("col")
    half, width = source.shape
    window = tau_ref.shape[1]
    keys = generators(count)
    tau_ref[:, :width] = source[...].astype(F32)
    lane = lax.broadcasted_iota(I32, (1, window), 1)
    owners = []
    for block in range(half // rows):
        flips = mask
        for step, key in enumerate(keys[:-2]):
            flips ^= key if (block >> step) & 1 else 0
        owners.append(me ^ flips)
    labels = jnp.concatenate(
        [label_ref[pl.ds(pl.multiple_of(owner * rows, rows), rows), :] for owner in owners], axis=0
    )[:, :1]
    places = [pl.ds(pl.multiple_of(lax.shift_right_logical(owner, 2) * rows, rows), rows) for owner in owners]

    def moved(i):
        place_at, size = table_ref[fields + 4 * i + 2], table_ref[fields + 4 * i + 3]
        return jnp.where((lane >= place_at) & (lane < place_at + size), pltpu.roll(tau_ref[...], place_at, 1), 0.0)

    def store(values):
        for block, to in enumerate(places):
            placed_ref[to, :] = values[block * rows:(block + 1) * rows]

    store(moved(0))

    @pl.loop(1, table_ref[1])
    def _(i):
        old = jnp.concatenate([placed_ref[to, :] for to in places], axis=0)
        store(jnp.where(labels == table_ref[fields + 4 * i].astype(F32), moved(i), old))


def near_kernel(count, rows, fields, table_ref, own_ref, other_ref, label_ref, after_ref, placed_ref, tau_ref):
    del after_ref
    for i, (mask, source) in enumerate(((0, own_ref), (generators(count)[-1], other_ref))):
        place(count, rows, mask, fields, table_ref, source, label_ref, tau_ref, placed_ref.at[i])


def far_kernel(count, rows, fields, table_ref, source_ref, label_ref, placed_ref, tau_ref):
    place(count, rows, generators(count)[-2], fields, table_ref, source_ref, label_ref, tau_ref, placed_ref)


def ladder_kernel(
    count, rows, total, tile, width, cd_rows, table_ref, last_ref, label_ref, near_ref, far_ref, early_ref, packed_ref, extra_ref, weight_ref,
    update_ref, energy_ref, tau_ref, other_ref, dense_ref, parts_ref,
):
    cols, pairs = weight_ref.shape
    window = tau_ref.shape[1]
    tiles = cols // tile
    fields, extras = fields_of(tiles, extra_ref.shape[0] - 1)
    keys = generators(count)
    place(count, rows, keys[-1] ^ keys[-2], fields, table_ref, last_ref, label_ref, tau_ref, other_ref)
    me = lax.axis_index("col")

    def block_of(owner):
        flips = me ^ owner
        other = flips & 1
        for bit in range(1, len(keys)):
            other = other ^ (lax.shift_right_logical(flips, bit) & 1)
        here = pl.ds(owner // 4 * rows, rows)
        away = jnp.where(other == 1, other_ref[here, :], far_ref[here, :])
        return jnp.where(flips & 2 == 2, away, near_ref[other, here, :])

    both = jnp.concatenate([block_of(owner) for owner in range(count)], axis=0)
    dense_ref[...] = both.astype(dense_ref.dtype)

    def integrals_of(t, size):
        early = early_ref.shape[0] // tile
        source, t = (early_ref, t) if t < early else (packed_ref, t - early)
        return source[t * tile:(t + 1) * tile, :size]

    row = lax.broadcasted_iota(I32, (tile, LANES), 0)
    row = jnp.concatenate([row] * (pairs // LANES), axis=1)

    def ladder_tile(integrals, begin, end, here, size):
        ladder = lax.dot_general(
            integrals, dense_ref[:, :size], (((1,), (1,)), ((), ())), preferred_element_type=F32
        )
        ladder = jnp.where((row >= begin) & (row < end) if begin is not None else row < end, ladder, 0.0)
        update = ladder * weight_ref[here, :]
        return update, jnp.sum((ladder * update).reshape(tile // 8, 8, pairs), axis=0)

    def extra_job(e, size):
        t, begin, end = (table_ref[extras + 4 * e + j] for j in (0, 2, 3))
        here = pl.ds(pl.multiple_of(t * tile, tile), tile)
        update, part = ladder_tile(extra_ref[e, :, :size], begin, end, here, size)
        update_ref[here, :] += update
        parts_ref[tiles + e] = part

    parts_ref[tiles + 1:] = jnp.zeros((parts_ref.shape[0] - tiles - 1,) + parts_ref.shape[1:], F32)
    for size in window_sizes(cd_rows, width):
        @pl.when(table_ref[0] == size)
        def _():
            for t in range(tiles):
                here = pl.ds(t * tile, tile)
                update_ref[here, :], parts_ref[t] = ladder_tile(
                    integrals_of(t, size), None, table_ref[4 + 2 * t], here, size
                )
            extra_job(0, size)

            @pl.loop(1, table_ref[2])
            def _(e):
                extra_job(e, size)

    energy_ref[...] = jnp.sum(jnp.sum(parts_ref[...], axis=0), axis=0, keepdims=True) / total


def shards(tau_packed, pair_irrep, cd_sizes, ab_sizes, integrals, occ_energy, virt_energy):
    cd_rows, cols = integrals.shape
    rows, width = tau_packed.shape
    pairs = pair_irrep.shape[0]
    irreps = cd_sizes.shape[0]
    count = lax.axis_size("col")
    keys = generators(count)
    tile = 160 if cols % 160 == 0 else cols
    tiles = cols // tile
    fields, extras = fields_of(tiles, irreps)
    window = window_of(width, cd_rows)
    entries = extras + 4 * (irreps + 1)

    early = (tiles * 6 // 10) * tile
    virt_row = virt_energy.reshape(1, cols)
    turned = far(integrals.T)
    held, table = pl.pallas_call(
        functools.partial(plan_kernel, tile, cd_rows, width, cols),
        out_shape=(pltpu.VMEM(tau_packed.shape, tau_packed.dtype), pltpu.SMEM((entries,), I32)),
        in_specs=[ANY] * 3,
        out_specs=(VMEM, SMEM),
        scratch_shapes=[
            pltpu.SMEM(cd_sizes.shape, I32), pltpu.SMEM(ab_sizes.shape, I32), pltpu.SemaphoreType.DMA((3,)),
        ],
        compiler_params=pltpu.CompilerParams(vmem_limit_bytes=1 << 20),
        cost_estimate=pl.CostEstimate(flops=0, bytes_accessed=1 << 20, transcendentals=0),
    )(far(tau_packed), far(cd_sizes), far(ab_sizes))
    table = pltpu.with_memory_space_constraint(table, pltpu.SMEM)
    sent = tau_packed
    for step, key in enumerate(keys[:-2]):
        held = jnp.concatenate([held, swap(sent, key, count)], axis=0)
        if step == 0:
            held, virt_row, occ_energy = lax.optimization_barrier((held, virt_row, occ_energy))
            weight, label, packed_early = pl.pallas_call(
                functools.partial(weight_kernel, tile, width),
                out_shape=(
                    pltpu.VMEM((cols, pairs), F32),
                    pltpu.VMEM((pairs, LANES), F32),
                    pltpu.VMEM((early, window), integrals.dtype),
                ),
                in_specs=[SMEM] + [ANY] * 3 + [VMEM, ANY],
                out_specs=(VMEM, VMEM, VMEM),
                scratch_shapes=[
                    pltpu.SMEM(ab_sizes.shape, I32),
                    pltpu.VMEM((1, pairs), I32),
                    pltpu.VMEM((1, pairs), F32),
                    pltpu.SemaphoreType.DMA((tiles,)),
                    pltpu.SemaphoreType.DMA((3,)),
                ],
                compiler_params=pltpu.CompilerParams(vmem_limit_bytes=2 << 20),
                cost_estimate=pl.CostEstimate(flops=10 * cols * pairs, bytes_accessed=4 * cols * pairs, transcendentals=0),
            )(
                table, far(ab_sizes), far(pair_irrep.reshape(1, pairs)), far(occ_energy.reshape(1, pairs)),
                near(virt_row), turned,
            )
        else:
            held = lax.optimization_barrier(held)
        sent = held
    held, label = lax.optimization_barrier((held, label))
    away = swap(held, keys[-2], count)
    other = swap(held, keys[-1], count)
    packed, extra, mark = pl.pallas_call(
        functools.partial(fetch_kernel, tile, width),
        out_shape=(
            pltpu.VMEM((cols - early, window), integrals.dtype),
            pltpu.VMEM((irreps + 1, tile, window), integrals.dtype),
            pltpu.VMEM((8, LANES), F32),
        ),
        in_specs=[SMEM, ANY, ANY],
        out_specs=(VMEM, VMEM, VMEM),
        scratch_shapes=[pltpu.SemaphoreType.DMA((tiles + irreps + 1,))],
        compiler_params=pltpu.CompilerParams(vmem_limit_bytes=1 << 20),
        cost_estimate=pl.CostEstimate(flops=0, bytes_accessed=2 * cols * width, transcendentals=0),
    )(table, near(label), turned)
    place_params = pltpu.CompilerParams(vmem_limit_bytes=(1 << 20) + 16 * pairs * window)
    place_cost = pl.CostEstimate(flops=10 * pairs * window, bytes_accessed=4 * pairs * window, transcendentals=0)
    quarter = pairs // 4
    placed_near = pl.pallas_call(
        functools.partial(near_kernel, count, rows, fields),
        out_shape=pltpu.VMEM((2, quarter, window), F32),
        in_specs=[SMEM, VMEM, VMEM, VMEM, ANY],
        out_specs=VMEM,
        scratch_shapes=[pltpu.VMEM((quarter, window), F32)],
        compiler_params=place_params,
        cost_estimate=place_cost,
    )(table, near(held), near(other), near(label), near(mark))
    away, placed_near = lax.optimization_barrier((away, placed_near))
    last = swap(away, keys[-1], count)
    placed_far = pl.pallas_call(
        functools.partial(far_kernel, count, rows, fields),
        out_shape=pltpu.VMEM((quarter, window), F32),
        in_specs=[SMEM, VMEM, VMEM],
        out_specs=VMEM,
        scratch_shapes=[pltpu.VMEM((quarter, window), F32)],
        compiler_params=place_params,
        cost_estimate=place_cost,
    )(table, near(away), near(label))
    update, energy = pl.pallas_call(
        functools.partial(ladder_kernel, count, rows, cols * count, tile, width, cd_rows),
        out_shape=(pltpu.VMEM((cols, pairs), F32), pltpu.VMEM((1, pairs), F32)),
        in_specs=[SMEM] + [VMEM] * 8,
        out_specs=(VMEM, VMEM),
        scratch_shapes=[
            pltpu.VMEM((quarter, window), F32),
            pltpu.VMEM((quarter, window), F32),
            pltpu.VMEM((pairs, window), jnp.bfloat16),
            pltpu.VMEM((tiles + irreps + 1, 8, pairs), F32),
        ],
        compiler_params=pltpu.CompilerParams(vmem_limit_bytes=(4 << 20) + 32 * pairs * window),
        cost_estimate=pl.CostEstimate(
            flops=2 * cols * width * pairs, bytes_accessed=2 * cols * width + 4 * cols * pairs, transcendentals=0
        ),
    )(table, near(last), near(label), near(placed_near), near(placed_far), near(packed_early), near(packed), near(extra), near(weight))
    for key in keys:
        energy = energy + swap(energy, key, count)
    return update.T, energy.reshape(pairs)


def solution(mesh):
    placed = (
        P(("job", "col"), None),
        P("job"),
        P("job"),
        P("job"),
        P("job", "col"),
        P("job"),
        P(("job", "col")),
    )
    return jax.shard_map(
        shards, mesh=mesh, in_specs=placed, out_specs=(P("job", "col"), P("job")), check_vma=False
    )
```

```python
import functools
import jax
import jax.numpy as jnp
from jax import lax
from jax.experimental import pallas as pl
from jax.experimental.pallas import tpu as pltpu
from jax.sharding import PartitionSpec as P

LANES = 128
F32 = jnp.float32
I32 = jnp.int32
VMEM = pl.BlockSpec(memory_space=pltpu.VMEM)
SMEM = pl.BlockSpec(memory_space=pltpu.SMEM)
ANY = pl.BlockSpec(memory_space=pl.ANY)


def generators(count):
    bits = count.bit_length() - 1
    return [(1 << b) | 1 for b in range(bits - 1, 0, -1)] + [1]


def swap(value, key, count):
    return lax.ppermute(value, "col", [(i, i ^ key) for i in range(count)])


def near(value):
    return pltpu.with_memory_space_constraint(value, pltpu.VMEM)


def far(value):
    return pltpu.with_memory_space_constraint(value, pltpu.HBM)


def window_of(width, cd_rows):
    return min(-(-(width + LANES - 1) // LANES) * LANES, cd_rows)


def window_sizes(cd_rows, width):
    most = window_of(width, cd_rows)
    return [size for size in range(256, most, 256)] + [most]


def fields_of(tiles, irreps):
    return 3 + 2 * tiles, 3 + 2 * tiles + 4 * (irreps + 1)


def plan(cd_ref, ab_ref, table_ref, me, cols, tile, cd_rows, width):
    sizes = window_sizes(cd_rows, width)
    tiles = cols // tile
    irreps = cd_ref.shape[0]
    fields, extras = fields_of(tiles, irreps)
    starts = [(jnp.int32(0), -me * cols)]
    for g in range(irreps):
        starts.append((starts[g][0] + cd_ref[g], starts[g][1] + ab_ref[g]))
    here = [(starts[g + 1][1] > 0) & (starts[g][1] < cols) for g in range(irreps)]
    most = jnp.int32(0)
    for g in range(irreps):
        need = lax.rem(starts[g][0], LANES) + cd_ref[g]
        most = jnp.maximum(most, jnp.where(here[g], need, 0))
    size = jnp.int32(sizes[-1])
    for choice in reversed(sizes):
        size = jnp.where(most <= choice, choice, size)
    present, extra = jnp.int32(0), jnp.int32(0)
    for g in range(irreps):
        cd_start, ab_start = starts[g]
        at = jnp.minimum(cd_start - lax.rem(cd_start, LANES), cd_rows - size)
        for j, value in enumerate((jnp.int32(g), at, cd_start - at, cd_ref[g])):
            table_ref[fields + 4 * present + j] = value
        inner = jnp.maximum(ab_start, 0)
        t = lax.div(inner, tile)
        for j, value in enumerate((t, present, inner - t * tile, starts[g + 1][1] - t * tile)):
            table_ref[extras + 4 * extra + j] = value
        extra = extra + jnp.where(here[g] & (lax.rem(inner, tile) > 0), 1, 0)
        present = present + jnp.where(here[g], 1, 0)
    for t in range(tiles):
        passed = jnp.int32(0)
        for g in range(irreps):
            passed = passed + jnp.where(here[g] & (starts[g + 1][1] <= t * tile), 1, 0)
        end = jnp.int32(tile)
        for g in reversed(range(irreps)):
            end = jnp.where(starts[g + 1][1] > t * tile, starts[g + 1][1] - t * tile, end)
        table_ref[3 + 2 * t] = passed
        table_ref[4 + 2 * t] = end
    for j in range(4):
        table_ref[extras + 4 * extra + j] = jnp.int32(0)
    table_ref[0] = size
    table_ref[1] = present
    table_ref[2] = extra


def plan_kernel(tile, cd_rows, width, cols, tau_ref, cd_hbm, ab_hbm, own_ref, table_ref, cd_ref, ab_ref, arrived):
    copies = [
        pltpu.make_async_copy(source, target, arrived.at[i])
        for i, (source, target) in enumerate(((cd_hbm, cd_ref), (ab_hbm, ab_ref)))
    ]
    for copy in copies:
        copy.start()
    own_ref[...] = tau_ref[...]
    for copy in copies:
        copy.wait()
    plan(cd_ref, ab_ref, table_ref, lax.axis_index("col"), cols, tile, cd_rows, width)


def tile_copies(tile, first, extras_at, table_ref, integrals_ref, packed_ref, extra_ref, arrived, size, act):
    fields, _ = fields_of(integrals_ref.shape[0] // tile, 0)
    count = packed_ref.shape[0] // tile

    def window(t, i):
        at = pl.multiple_of(table_ref[fields + 4 * i + 1], LANES)
        return integrals_ref.at[pl.ds(pl.multiple_of(t * tile, tile), tile), pl.ds(at, size)]

    @pl.loop(0, count)
    def _(t):
        to = packed_ref.at[pl.ds(pl.multiple_of(t * tile, tile), tile), pl.ds(0, size)]
        act(pltpu.make_async_copy(window(first + t, table_ref[3 + 2 * (first + t)]), to, arrived.at[t]))

    if extra_ref is not None:
        @pl.loop(0, table_ref[2])
        def _(e):
            source = window(table_ref[extras_at + 4 * e], table_ref[extras_at + 4 * e + 1])
            act(pltpu.make_async_copy(source, extra_ref.at[e, :, pl.ds(0, size)], arrived.at[count + e]))


def weight_kernel(
    tile, width, table_ref, ab_hbm, irrep_hbm, occ_hbm, virt_hbm, integrals_ref,
    weight_ref, label_ref, packed_ref, ab_ref, irrep_ref, occ_ref, virt_ref, arrived, here,
):
    copies = [
        pltpu.make_async_copy(source, target, here.at[i])
        for i, (source, target) in enumerate(
            ((ab_hbm, ab_ref), (irrep_hbm, irrep_ref), (occ_hbm, occ_ref), (virt_hbm, virt_ref))
        )
    ]
    for copy in copies:
        copy.start()
    cols, cd_rows = integrals_ref.shape
    pairs = weight_ref.shape[1]

    def each_copy(act):
        for size in window_sizes(cd_rows, width):
            @pl.when(table_ref[0] == size)
            def _():
                tile_copies(tile, 0, 0, table_ref, integrals_ref, packed_ref, None, arrived, size, act)

    each_copy(lambda copy: copy.start())
    for copy in copies:
        copy.wait()
    label = irrep_ref[...]
    low = jnp.zeros((1, pairs), I32)
    high = jnp.zeros((1, pairs), I32)
    start = -lax.axis_index("col") * cols
    for g in range(ab_ref.shape[0]):
        end = start + ab_ref[g]
        low = jnp.where(label == g, start, low)
        high = jnp.where(label == g, end, high)
        start = end
    occ = occ_ref[...]
    for c in range(0, cols, LANES):
        span = min(LANES, cols - c)
        virt = jnp.transpose(jnp.broadcast_to(virt_ref[c:c + span].reshape(1, span), (LANES, span)))
        at = c + lax.broadcasted_iota(I32, (span, LANES), 0)
        for p in range(0, pairs, LANES):
            lanes = slice(p, p + LANES)
            keep = (at >= low[:, lanes]) & (at < high[:, lanes])
            weight_ref[c:c + span, lanes] = jnp.where(keep, 1.0 / (virt - occ[:, lanes]), 0.0)
    for p in range(0, pairs, LANES):
        label_ref[p:p + LANES, :] = jnp.transpose(jnp.broadcast_to(label[:, p:p + LANES].astype(F32), (LANES, LANES)))
    each_copy(lambda copy: copy.wait())


def fetch_kernel(tile, width, table_ref, after_ref, integrals_ref, packed_ref, extra_ref, mark_ref, arrived):
    del after_ref
    cols, cd_rows = integrals_ref.shape
    first = (cols - packed_ref.shape[0]) // tile
    _, extras_at = fields_of(cols // tile, extra_ref.shape[0] - 1)
    for size in window_sizes(cd_rows, width):
        @pl.when(table_ref[0] == size)
        def _():
            args = (tile, first, extras_at, table_ref, integrals_ref, packed_ref, extra_ref, arrived, size)
            tile_copies(*args, lambda copy: copy.start())
            tile_copies(*args, lambda copy: copy.wait())
    mark_ref[...] = jnp.zeros(mark_ref.shape, F32)


def place(count, rows, mask, fields, table_ref, source, label_ref, tau_ref, placed_ref):
    me = lax.axis_index("col")
    half, width = source.shape
    window = tau_ref.shape[1]
    keys = generators(count)
    tau_ref[:, :width] = source[...].astype(F32)
    lane = lax.broadcasted_iota(I32, (1, window), 1)
    owners = []
    for block in range(half // rows):
        flips = mask
        for step, key in enumerate(keys[:-2]):
            flips ^= key if (block >> step) & 1 else 0
        owners.append(me ^ flips)
    labels = jnp.concatenate(
        [label_ref[pl.ds(pl.multiple_of(owner * rows, rows), rows), :] for owner in owners], axis=0
    )[:, :1]
    places = [pl.ds(pl.multiple_of(lax.shift_right_logical(owner, 2) * rows, rows), rows) for owner in owners]

    def moved(i):
        place_at, size = table_ref[fields + 4 * i + 2], table_ref[fields + 4 * i + 3]
        return jnp.where((lane >= place_at) & (lane < place_at + size), pltpu.roll(tau_ref[...], place_at, 1), 0.0)

    def store(values):
        for block, to in enumerate(places):
            placed_ref[to, :] = values[block * rows:(block + 1) * rows]

    store(moved(0))

    @pl.loop(1, table_ref[1])
    def _(i):
        old = jnp.concatenate([placed_ref[to, :] for to in places], axis=0)
        store(jnp.where(labels == table_ref[fields + 4 * i].astype(F32), moved(i), old))


def near_kernel(count, rows, fields, table_ref, own_ref, other_ref, label_ref, after_ref, placed_ref, tau_ref):
    del after_ref
    for i, (mask, source) in enumerate(((0, own_ref), (generators(count)[-1], other_ref))):
        place(count, rows, mask, fields, table_ref, source, label_ref, tau_ref, placed_ref.at[i])


def far_kernel(count, rows, fields, table_ref, source_ref, label_ref, placed_ref, tau_ref):
    place(count, rows, generators(count)[-2], fields, table_ref, source_ref, label_ref, tau_ref, placed_ref)


def ladder_kernel(
    count, rows, total, tile, width, cd_rows, table_ref, last_ref, label_ref, near_ref, far_ref, early_ref, packed_ref, extra_ref, weight_ref,
    update_ref, energy_ref, tau_ref, other_ref, dense_ref, parts_ref,
):
    cols, pairs = weight_ref.shape
    window = tau_ref.shape[1]
    tiles = cols // tile
    fields, extras = fields_of(tiles, extra_ref.shape[0] - 1)
    keys = generators(count)
    place(count, rows, keys[-1] ^ keys[-2], fields, table_ref, last_ref, label_ref, tau_ref, other_ref)
    me = lax.axis_index("col")

    def block_of(owner):
        flips = me ^ owner
        other = flips & 1
        for bit in range(1, len(keys)):
            other = other ^ (lax.shift_right_logical(flips, bit) & 1)
        here = pl.ds(owner // 4 * rows, rows)
        away = jnp.where(other == 1, other_ref[here, :], far_ref[here, :])
        return jnp.where(flips & 2 == 2, away, near_ref[other, here, :])

    both = jnp.concatenate([block_of(owner) for owner in range(count)], axis=0)
    dense_ref[...] = both.astype(dense_ref.dtype)

    def integrals_of(t, size):
        early = early_ref.shape[0] // tile
        source, t = (early_ref, t) if t < early else (packed_ref, t - early)
        return source[t * tile:(t + 1) * tile, :size]

    row = lax.broadcasted_iota(I32, (tile, LANES), 0)
    row = jnp.concatenate([row] * (pairs // LANES), axis=1)

    def ladder_tile(integrals, begin, end, here, size):
        ladder = lax.dot_general(
            integrals, dense_ref[:, :size], (((1,), (1,)), ((), ())), preferred_element_type=F32
        )
        ladder = jnp.where((row >= begin) & (row < end) if begin is not None else row < end, ladder, 0.0)
        update = ladder * weight_ref[here, :]
        return update, jnp.sum((ladder * update).reshape(tile // 8, 8, pairs), axis=0)

    def extra_job(e, size):
        t, begin, end = (table_ref[extras + 4 * e + j] for j in (0, 2, 3))
        here = pl.ds(pl.multiple_of(t * tile, tile), tile)
        update, part = ladder_tile(extra_ref[e, :, :size], begin, end, here, size)
        update_ref[here, :] += update
        parts_ref[tiles + e] = part

    parts_ref[tiles + 1:] = jnp.zeros((parts_ref.shape[0] - tiles - 1,) + parts_ref.shape[1:], F32)
    for size in window_sizes(cd_rows, width):
        @pl.when(table_ref[0] == size)
        def _():
            for t in range(tiles):
                here = pl.ds(t * tile, tile)
                update_ref[here, :], parts_ref[t] = ladder_tile(
                    integrals_of(t, size), None, table_ref[4 + 2 * t], here, size
                )
            extra_job(0, size)

            @pl.loop(1, table_ref[2])
            def _(e):
                extra_job(e, size)

    energy_ref[...] = jnp.sum(jnp.sum(parts_ref[...], axis=0), axis=0, keepdims=True) / total


def shards(tau_packed, pair_irrep, cd_sizes, ab_sizes, integrals, occ_energy, virt_energy):
    cd_rows, cols = integrals.shape
    rows, width = tau_packed.shape
    pairs = pair_irrep.shape[0]
    irreps = cd_sizes.shape[0]
    count = lax.axis_size("col")
    keys = generators(count)
    tile = 160 if cols % 160 == 0 else cols
    tiles = cols // tile
    fields, extras = fields_of(tiles, irreps)
    window = window_of(width, cd_rows)
    entries = extras + 4 * (irreps + 1)

    early = (tiles // 2) * tile
    turned = far(integrals.T)
    held, table = pl.pallas_call(
        functools.partial(plan_kernel, tile, cd_rows, width, cols),
        out_shape=(pltpu.VMEM(tau_packed.shape, tau_packed.dtype), pltpu.SMEM((entries,), I32)),
        in_specs=[VMEM, ANY, ANY],
        out_specs=(VMEM, SMEM),
        scratch_shapes=[
            pltpu.SMEM(cd_sizes.shape, I32), pltpu.SMEM(ab_sizes.shape, I32), pltpu.SemaphoreType.DMA((2,)),
        ],
        compiler_params=pltpu.CompilerParams(vmem_limit_bytes=1 << 20),
        cost_estimate=pl.CostEstimate(flops=0, bytes_accessed=1 << 20, transcendentals=0),
    )(tau_packed, far(cd_sizes), far(ab_sizes))
    table = pltpu.with_memory_space_constraint(table, pltpu.SMEM)
    sent = tau_packed
    for step, key in enumerate(keys[:-2]):
        held = jnp.concatenate([held, swap(sent, key, count)], axis=0)
        if step == 0:
            held, occ_energy = lax.optimization_barrier((held, occ_energy))
            weight, label, packed_early = pl.pallas_call(
                functools.partial(weight_kernel, tile, width),
                out_shape=(
                    pltpu.VMEM((cols, pairs), F32),
                    pltpu.VMEM((pairs, LANES), F32),
                    pltpu.VMEM((early, window), integrals.dtype),
                ),
                in_specs=[SMEM] + [ANY] * 5,
                out_specs=(VMEM, VMEM, VMEM),
                scratch_shapes=[
                    pltpu.SMEM(ab_sizes.shape, I32),
                    pltpu.VMEM((1, pairs), I32),
                    pltpu.VMEM((1, pairs), F32),
                    pltpu.VMEM((cols,), F32),
                    pltpu.SemaphoreType.DMA((tiles,)),
                    pltpu.SemaphoreType.DMA((4,)),
                ],
                compiler_params=pltpu.CompilerParams(vmem_limit_bytes=2 << 20),
                cost_estimate=pl.CostEstimate(flops=10 * cols * pairs, bytes_accessed=4 * cols * pairs, transcendentals=0),
            )(
                table, far(ab_sizes), far(pair_irrep.reshape(1, pairs)), far(occ_energy.reshape(1, pairs)),
                far(virt_energy), turned,
            )
        else:
            held = lax.optimization_barrier(held)
        sent = held
    held, label = lax.optimization_barrier((held, label))
    away = swap(held, keys[-2], count)
    other = swap(held, keys[-1], count)
    packed, extra, mark = pl.pallas_call(
        functools.partial(fetch_kernel, tile, width),
        out_shape=(
            pltpu.VMEM((cols - early, window), integrals.dtype),
            pltpu.VMEM((irreps + 1, tile, window), integrals.dtype),
            pltpu.VMEM((8, LANES), F32),
        ),
        in_specs=[SMEM, ANY, ANY],
        out_specs=(VMEM, VMEM, VMEM),
        scratch_shapes=[pltpu.SemaphoreType.DMA((tiles + irreps + 1,))],
        compiler_params=pltpu.CompilerParams(vmem_limit_bytes=1 << 20),
        cost_estimate=pl.CostEstimate(flops=0, bytes_accessed=2 * cols * width, transcendentals=0),
    )(table, near(label), turned)
    place_params = pltpu.CompilerParams(vmem_limit_bytes=(1 << 20) + 16 * pairs * window)
    place_cost = pl.CostEstimate(flops=10 * pairs * window, bytes_accessed=4 * pairs * window, transcendentals=0)
    quarter = pairs // 4
    placed_near = pl.pallas_call(
        functools.partial(near_kernel, count, rows, fields),
        out_shape=pltpu.VMEM((2, quarter, window), F32),
        in_specs=[SMEM, VMEM, VMEM, VMEM, ANY],
        out_specs=VMEM,
        scratch_shapes=[pltpu.VMEM((quarter, window), F32)],
        compiler_params=place_params,
        cost_estimate=place_cost,
    )(table, near(held), near(other), near(label), near(mark))
    away, placed_near = lax.optimization_barrier((away, placed_near))
    last = swap(away, keys[-1], count)
    placed_far = pl.pallas_call(
        functools.partial(far_kernel, count, rows, fields),
        out_shape=pltpu.VMEM((quarter, window), F32),
        in_specs=[SMEM, VMEM, VMEM],
        out_specs=VMEM,
        scratch_shapes=[pltpu.VMEM((quarter, window), F32)],
        compiler_params=place_params,
        cost_estimate=place_cost,
    )(table, near(away), near(label))
    update, energy = pl.pallas_call(
        functools.partial(ladder_kernel, count, rows, cols * count, tile, width, cd_rows),
        out_shape=(pltpu.VMEM((cols, pairs), F32), pltpu.VMEM((1, pairs), F32)),
        in_specs=[SMEM] + [VMEM] * 8,
        out_specs=(VMEM, VMEM),
        scratch_shapes=[
            pltpu.VMEM((quarter, window), F32),
            pltpu.VMEM((quarter, window), F32),
            pltpu.VMEM((pairs, window), jnp.bfloat16),
            pltpu.VMEM((tiles + irreps + 1, 8, pairs), F32),
        ],
        compiler_params=pltpu.CompilerParams(vmem_limit_bytes=(4 << 20) + 32 * pairs * window),
        cost_estimate=pl.CostEstimate(
            flops=2 * cols * width * pairs, bytes_accessed=2 * cols * width + 4 * cols * pairs, transcendentals=0
        ),
    )(table, near(last), near(label), near(placed_near), near(placed_far), near(packed_early), near(packed), near(extra), near(weight))
    for key in keys:
        energy = energy + swap(energy, key, count)
    return update.T, energy.reshape(pairs)


def solution(mesh):
    placed = (
        P(("job", "col"), None),
        P("job"),
        P("job"),
        P("job"),
        P("job", "col"),
        P("job"),
        P(("job", "col")),
    )
    return jax.shard_map(
        shards, mesh=mesh, in_specs=placed, out_specs=(P("job", "col"), P("job")), check_vma=False
    )
```

```python
import functools
import jax
import jax.numpy as jnp
from jax import lax
from jax.experimental import pallas as pl
from jax.experimental.pallas import tpu as pltpu
from jax.sharding import PartitionSpec as P

LANES = 128
F32 = jnp.float32
I32 = jnp.int32
VMEM = pl.BlockSpec(memory_space=pltpu.VMEM)
SMEM = pl.BlockSpec(memory_space=pltpu.SMEM)
ANY = pl.BlockSpec(memory_space=pl.ANY)


def generators(count):
    bits = count.bit_length() - 1
    return [(1 << b) | 1 for b in range(bits - 1, 0, -1)] + [1]


def swap(value, key, count):
    return lax.ppermute(value, "col", [(i, i ^ key) for i in range(count)])


def near(value):
    return pltpu.with_memory_space_constraint(value, pltpu.VMEM)


def far(value):
    return pltpu.with_memory_space_constraint(value, pltpu.HBM)


def window_of(width, cd_rows):
    return min(-(-(width + LANES - 1) // LANES) * LANES, cd_rows)


def window_sizes(cd_rows, width):
    most = window_of(width, cd_rows)
    return [size for size in range(256, most, 256)] + [most]


def fields_of(tiles, irreps):
    return 3 + 2 * tiles, 3 + 2 * tiles + 4 * (irreps + 1)


def plan(cd_ref, ab_ref, table_ref, me, cols, tile, cd_rows, width):
    sizes = window_sizes(cd_rows, width)
    tiles = cols // tile
    irreps = cd_ref.shape[0]
    fields, extras = fields_of(tiles, irreps)
    starts = [(jnp.int32(0), -me * cols)]
    for g in range(irreps):
        starts.append((starts[g][0] + cd_ref[g], starts[g][1] + ab_ref[g]))
    here = [(starts[g + 1][1] > 0) & (starts[g][1] < cols) for g in range(irreps)]
    most = jnp.int32(0)
    for g in range(irreps):
        need = lax.rem(starts[g][0], LANES) + cd_ref[g]
        most = jnp.maximum(most, jnp.where(here[g], need, 0))
    size = jnp.int32(sizes[-1])
    for choice in reversed(sizes):
        size = jnp.where(most <= choice, choice, size)
    present, extra = jnp.int32(0), jnp.int32(0)
    for g in range(irreps):
        cd_start, ab_start = starts[g]
        at = jnp.minimum(cd_start - lax.rem(cd_start, LANES), cd_rows - size)
        for j, value in enumerate((jnp.int32(g), at, cd_start - at, cd_ref[g])):
            table_ref[fields + 4 * present + j] = value
        inner = jnp.maximum(ab_start, 0)
        t = lax.div(inner, tile)
        for j, value in enumerate((t, present, inner - t * tile, starts[g + 1][1] - t * tile)):
            table_ref[extras + 4 * extra + j] = value
        extra = extra + jnp.where(here[g] & (lax.rem(inner, tile) > 0), 1, 0)
        present = present + jnp.where(here[g], 1, 0)
    for t in range(tiles):
        passed = jnp.int32(0)
        for g in range(irreps):
            passed = passed + jnp.where(here[g] & (starts[g + 1][1] <= t * tile), 1, 0)
        end = jnp.int32(tile)
        for g in reversed(range(irreps)):
            end = jnp.where(starts[g + 1][1] > t * tile, starts[g + 1][1] - t * tile, end)
        table_ref[3 + 2 * t] = passed
        table_ref[4 + 2 * t] = end
    for j in range(4):
        table_ref[extras + 4 * extra + j] = jnp.int32(0)
    table_ref[0] = size
    table_ref[1] = present
    table_ref[2] = extra


def plan_kernel(tile, cd_rows, width, cols, tau_ref, cd_hbm, ab_hbm, own_ref, table_ref, cd_ref, ab_ref, arrived):
    copies = [
        pltpu.make_async_copy(source, target, arrived.at[i])
        for i, (source, target) in enumerate(((cd_hbm, cd_ref), (ab_hbm, ab_ref)))
    ]
    for copy in copies:
        copy.start()
    own_ref[...] = tau_ref[...]
    for copy in copies:
        copy.wait()
    plan(cd_ref, ab_ref, table_ref, lax.axis_index("col"), cols, tile, cd_rows, width)


def tile_copies(tile, first, extras_at, table_ref, integrals_ref, packed_ref, extra_ref, arrived, size, act):
    fields, _ = fields_of(integrals_ref.shape[0] // tile, 0)
    count = packed_ref.shape[0] // tile

    def window(t, i):
        at = pl.multiple_of(table_ref[fields + 4 * i + 1], LANES)
        return integrals_ref.at[pl.ds(pl.multiple_of(t * tile, tile), tile), pl.ds(at, size)]

    @pl.loop(0, count)
    def _(t):
        to = packed_ref.at[pl.ds(pl.multiple_of(t * tile, tile), tile), pl.ds(0, size)]
        act(pltpu.make_async_copy(window(first + t, table_ref[3 + 2 * (first + t)]), to, arrived.at[t]))

    if extra_ref is not None:
        @pl.loop(0, table_ref[2])
        def _(e):
            source = window(table_ref[extras_at + 4 * e], table_ref[extras_at + 4 * e + 1])
            act(pltpu.make_async_copy(source, extra_ref.at[e, :, pl.ds(0, size)], arrived.at[count + e]))


def weight_kernel(
    tile, width, table_ref, ab_hbm, irrep_hbm, occ_hbm, virt_hbm, integrals_ref,
    weight_ref, label_ref, packed_ref, ab_ref, irrep_ref, occ_ref, virt_ref, arrived, here,
):
    copies = [
        pltpu.make_async_copy(source, target, here.at[i])
        for i, (source, target) in enumerate(
            ((ab_hbm, ab_ref), (irrep_hbm, irrep_ref), (occ_hbm, occ_ref), (virt_hbm, virt_ref))
        )
    ]
    for copy in copies:
        copy.start()
    cols, cd_rows = integrals_ref.shape
    pairs = weight_ref.shape[1]

    def each_copy(act):
        for size in window_sizes(cd_rows, width):
            @pl.when(table_ref[0] == size)
            def _():
                tile_copies(tile, 0, 0, table_ref, integrals_ref, packed_ref, None, arrived, size, act)

    each_copy(lambda copy: copy.start())
    for copy in copies:
        copy.wait()
    label = irrep_ref[...]
    low = jnp.zeros((1, pairs), I32)
    high = jnp.zeros((1, pairs), I32)
    start = -lax.axis_index("col") * cols
    for g in range(ab_ref.shape[0]):
        end = start + ab_ref[g]
        low = jnp.where(label == g, start, low)
        high = jnp.where(label == g, end, high)
        start = end
    occ = occ_ref[...]
    for c in range(0, cols, LANES):
        span = min(LANES, cols - c)
        virt = jnp.transpose(jnp.broadcast_to(virt_ref[c:c + span].reshape(1, span), (LANES, span)))
        at = c + lax.broadcasted_iota(I32, (span, LANES), 0)
        for p in range(0, pairs, LANES):
            lanes = slice(p, p + LANES)
            keep = (at >= low[:, lanes]) & (at < high[:, lanes])
            weight_ref[c:c + span, lanes] = jnp.where(keep, 1.0 / (virt - occ[:, lanes]), 0.0)
    for p in range(0, pairs, LANES):
        label_ref[p:p + LANES, :] = jnp.transpose(jnp.broadcast_to(label[:, p:p + LANES].astype(F32), (LANES, LANES)))
    each_copy(lambda copy: copy.wait())


def fetch_kernel(tile, width, table_ref, after_ref, integrals_ref, packed_ref, extra_ref, mark_ref, arrived):
    del after_ref
    cols, cd_rows = integrals_ref.shape
    first = (cols - packed_ref.shape[0]) // tile
    _, extras_at = fields_of(cols // tile, extra_ref.shape[0] - 1)
    for size in window_sizes(cd_rows, width):
        @pl.when(table_ref[0] == size)
        def _():
            args = (tile, first, extras_at, table_ref, integrals_ref, packed_ref, extra_ref, arrived, size)
            tile_copies(*args, lambda copy: copy.start())
            tile_copies(*args, lambda copy: copy.wait())
    mark_ref[...] = jnp.zeros(mark_ref.shape, F32)


def place(count, rows, mask, fields, table_ref, source, label_ref, tau_ref, placed_ref):
    me = lax.axis_index("col")
    half, width = source.shape
    window = tau_ref.shape[1] // 2
    keys = generators(count)
    tau_ref[:, window:window + width] = source[...].astype(F32)
    lane = lax.broadcasted_iota(I32, (1, window), 1)
    owners = []
    for block in range(half // rows):
        flips = mask
        for step, key in enumerate(keys[:-2]):
            flips ^= key if (block >> step) & 1 else 0
        owners.append(me ^ flips)
    labels = jnp.concatenate(
        [label_ref[pl.ds(pl.multiple_of(owner * rows, rows), rows), :] for owner in owners], axis=0
    )[:, :1]
    places = [pl.ds(pl.multiple_of(lax.shift_right_logical(owner, 2) * rows, rows), rows) for owner in owners]

    def moved(i):
        place_at, size = table_ref[fields + 4 * i + 2], table_ref[fields + 4 * i + 3]
        turn = lax.rem(place_at, LANES)
        values = tau_ref[:, pl.ds(pl.multiple_of(window + turn - place_at, LANES), window)]
        pieces = [pltpu.roll(values[:, c:c + LANES], turn, 1) for c in range(0, window, LANES)]
        wrapped = lane[:, :LANES] < turn
        shifted = [jnp.where(wrapped, before, piece) for before, piece in zip(pieces[-1:] + pieces[:-1], pieces)]
        return jnp.where((lane >= place_at) & (lane < place_at + size), jnp.concatenate(shifted, axis=1), 0.0)

    def store(values):
        for block, to in enumerate(places):
            placed_ref[to, :] = values[block * rows:(block + 1) * rows]

    store(moved(0))

    @pl.loop(1, table_ref[1])
    def _(i):
        old = jnp.concatenate([placed_ref[to, :] for to in places], axis=0)
        store(jnp.where(labels == table_ref[fields + 4 * i].astype(F32), moved(i), old))


def near_kernel(count, rows, fields, table_ref, own_ref, other_ref, label_ref, after_ref, placed_ref, tau_ref):
    del after_ref
    for i, (mask, source) in enumerate(((0, own_ref), (generators(count)[-1], other_ref))):
        place(count, rows, mask, fields, table_ref, source, label_ref, tau_ref, placed_ref.at[i])


def far_kernel(count, rows, fields, table_ref, source_ref, label_ref, placed_ref, tau_ref):
    place(count, rows, generators(count)[-2], fields, table_ref, source_ref, label_ref, tau_ref, placed_ref)


def ladder_kernel(
    count, rows, total, tile, width, cd_rows, table_ref, last_ref, label_ref, near_ref, far_ref, early_ref, packed_ref, extra_ref, weight_ref,
    update_ref, energy_ref, tau_ref, other_ref, dense_ref, parts_ref,
):
    cols, pairs = weight_ref.shape
    tiles = cols // tile
    fields, extras = fields_of(tiles, extra_ref.shape[0] - 1)
    keys = generators(count)
    place(count, rows, keys[-1] ^ keys[-2], fields, table_ref, last_ref, label_ref, tau_ref, other_ref)
    me = lax.axis_index("col")

    def block_of(owner):
        flips = me ^ owner
        other = flips & 1
        for bit in range(1, len(keys)):
            other = other ^ (lax.shift_right_logical(flips, bit) & 1)
        here = pl.ds(owner // 4 * rows, rows)
        away = jnp.where(other == 1, other_ref[here, :], far_ref[here, :])
        return jnp.where(flips & 2 == 2, away, near_ref[other, here, :])

    both = jnp.concatenate([block_of(owner) for owner in range(count)], axis=0)
    dense_ref[...] = both.astype(dense_ref.dtype)

    def integrals_of(t, size):
        early = early_ref.shape[0] // tile
        source, t = (early_ref, t) if t < early else (packed_ref, t - early)
        return source[t * tile:(t + 1) * tile, :size]

    row = lax.broadcasted_iota(I32, (tile, LANES), 0)
    row = jnp.concatenate([row] * (pairs // LANES), axis=1)

    def ladder_tile(integrals, begin, end, here, size):
        ladder = lax.dot_general(
            integrals, dense_ref[:, :size], (((1,), (1,)), ((), ())), preferred_element_type=F32
        )
        ladder = jnp.where((row >= begin) & (row < end) if begin is not None else row < end, ladder, 0.0)
        update = ladder * weight_ref[here, :]
        return update, jnp.sum((ladder * update).reshape(tile // 8, 8, pairs), axis=0)

    def extra_job(e, size):
        t, begin, end = (table_ref[extras + 4 * e + j] for j in (0, 2, 3))
        here = pl.ds(pl.multiple_of(t * tile, tile), tile)
        update, part = ladder_tile(extra_ref[e, :, :size], begin, end, here, size)
        update_ref[here, :] += update
        parts_ref[tiles + e] = part

    parts_ref[tiles + 1:] = jnp.zeros((parts_ref.shape[0] - tiles - 1,) + parts_ref.shape[1:], F32)
    for size in window_sizes(cd_rows, width):
        @pl.when(table_ref[0] == size)
        def _():
            for t in range(tiles):
                here = pl.ds(t * tile, tile)
                update_ref[here, :], parts_ref[t] = ladder_tile(
                    integrals_of(t, size), None, table_ref[4 + 2 * t], here, size
                )
            extra_job(0, size)

            @pl.loop(1, table_ref[2])
            def _(e):
                extra_job(e, size)

    energy_ref[...] = jnp.sum(jnp.sum(parts_ref[...], axis=0), axis=0, keepdims=True) / total


def shards(tau_packed, pair_irrep, cd_sizes, ab_sizes, integrals, occ_energy, virt_energy):
    cd_rows, cols = integrals.shape
    rows, width = tau_packed.shape
    pairs = pair_irrep.shape[0]
    irreps = cd_sizes.shape[0]
    count = lax.axis_size("col")
    keys = generators(count)
    tile = 160 if cols % 160 == 0 else cols
    tiles = cols // tile
    fields, extras = fields_of(tiles, irreps)
    window = window_of(width, cd_rows)
    entries = extras + 4 * (irreps + 1)

    early = (tiles // 2) * tile
    turned = far(integrals.T)
    held, table = pl.pallas_call(
        functools.partial(plan_kernel, tile, cd_rows, width, cols),
        out_shape=(pltpu.VMEM(tau_packed.shape, tau_packed.dtype), pltpu.SMEM((entries,), I32)),
        in_specs=[VMEM, ANY, ANY],
        out_specs=(VMEM, SMEM),
        scratch_shapes=[
            pltpu.SMEM(cd_sizes.shape, I32), pltpu.SMEM(ab_sizes.shape, I32), pltpu.SemaphoreType.DMA((2,)),
        ],
        compiler_params=pltpu.CompilerParams(vmem_limit_bytes=1 << 20),
        cost_estimate=pl.CostEstimate(flops=0, bytes_accessed=1 << 20, transcendentals=0),
    )(tau_packed, far(cd_sizes), far(ab_sizes))
    table = pltpu.with_memory_space_constraint(table, pltpu.SMEM)
    sent = tau_packed
    for step, key in enumerate(keys[:-2]):
        held = jnp.concatenate([held, swap(sent, key, count)], axis=0)
        if step == 0:
            held, occ_energy = lax.optimization_barrier((held, occ_energy))
            weight, label, packed_early = pl.pallas_call(
                functools.partial(weight_kernel, tile, width),
                out_shape=(
                    pltpu.VMEM((cols, pairs), F32),
                    pltpu.VMEM((pairs, LANES), F32),
                    pltpu.VMEM((early, window), integrals.dtype),
                ),
                in_specs=[SMEM] + [ANY] * 5,
                out_specs=(VMEM, VMEM, VMEM),
                scratch_shapes=[
                    pltpu.SMEM(ab_sizes.shape, I32),
                    pltpu.VMEM((1, pairs), I32),
                    pltpu.VMEM((1, pairs), F32),
                    pltpu.VMEM((cols,), F32),
                    pltpu.SemaphoreType.DMA((tiles,)),
                    pltpu.SemaphoreType.DMA((4,)),
                ],
                compiler_params=pltpu.CompilerParams(vmem_limit_bytes=2 << 20),
                cost_estimate=pl.CostEstimate(flops=10 * cols * pairs, bytes_accessed=4 * cols * pairs, transcendentals=0),
            )(
                table, far(ab_sizes), far(pair_irrep.reshape(1, pairs)), far(occ_energy.reshape(1, pairs)),
                far(virt_energy), turned,
            )
        else:
            held = lax.optimization_barrier(held)
        sent = held
    held, label = lax.optimization_barrier((held, label))
    away = swap(held, keys[-2], count)
    other = swap(held, keys[-1], count)
    packed, extra, mark = pl.pallas_call(
        functools.partial(fetch_kernel, tile, width),
        out_shape=(
            pltpu.VMEM((cols - early, window), integrals.dtype),
            pltpu.VMEM((irreps + 1, tile, window), integrals.dtype),
            pltpu.VMEM((8, LANES), F32),
        ),
        in_specs=[SMEM, ANY, ANY],
        out_specs=(VMEM, VMEM, VMEM),
        scratch_shapes=[pltpu.SemaphoreType.DMA((tiles + irreps + 1,))],
        compiler_params=pltpu.CompilerParams(vmem_limit_bytes=1 << 20),
        cost_estimate=pl.CostEstimate(flops=0, bytes_accessed=2 * cols * width, transcendentals=0),
    )(table, near(label), turned)
    place_params = pltpu.CompilerParams(vmem_limit_bytes=(1 << 20) + 16 * pairs * window)
    place_cost = pl.CostEstimate(flops=10 * pairs * window, bytes_accessed=4 * pairs * window, transcendentals=0)
    quarter = pairs // 4
    placed_near = pl.pallas_call(
        functools.partial(near_kernel, count, rows, fields),
        out_shape=pltpu.VMEM((2, quarter, window), F32),
        in_specs=[SMEM, VMEM, VMEM, VMEM, ANY],
        out_specs=VMEM,
        scratch_shapes=[pltpu.VMEM((quarter, 2 * window), F32)],
        compiler_params=place_params,
        cost_estimate=place_cost,
    )(table, near(held), near(other), near(label), near(mark))
    away, placed_near = lax.optimization_barrier((away, placed_near))
    last = swap(away, keys[-1], count)
    placed_far = pl.pallas_call(
        functools.partial(far_kernel, count, rows, fields),
        out_shape=pltpu.VMEM((quarter, window), F32),
        in_specs=[SMEM, VMEM, VMEM],
        out_specs=VMEM,
        scratch_shapes=[pltpu.VMEM((quarter, 2 * window), F32)],
        compiler_params=place_params,
        cost_estimate=place_cost,
    )(table, near(away), near(label))
    update, energy = pl.pallas_call(
        functools.partial(ladder_kernel, count, rows, cols * count, tile, width, cd_rows),
        out_shape=(pltpu.VMEM((cols, pairs), F32), pltpu.VMEM((1, pairs), F32)),
        in_specs=[SMEM] + [VMEM] * 8,
        out_specs=(VMEM, VMEM),
        scratch_shapes=[
            pltpu.VMEM((quarter, 2 * window), F32),
            pltpu.VMEM((quarter, window), F32),
            pltpu.VMEM((pairs, window), jnp.bfloat16),
            pltpu.VMEM((tiles + irreps + 1, 8, pairs), F32),
        ],
        compiler_params=pltpu.CompilerParams(vmem_limit_bytes=(4 << 20) + 32 * pairs * window),
        cost_estimate=pl.CostEstimate(
            flops=2 * cols * width * pairs, bytes_accessed=2 * cols * width + 4 * cols * pairs, transcendentals=0
        ),
    )(table, near(last), near(label), near(placed_near), near(placed_far), near(packed_early), near(packed), near(extra), near(weight))
    for key in keys:
        energy = energy + swap(energy, key, count)
    return update.T, energy.reshape(pairs)


def solution(mesh):
    placed = (
        P(("job", "col"), None),
        P("job"),
        P("job"),
        P("job"),
        P("job", "col"),
        P("job"),
        P(("job", "col")),
    )
    return jax.shard_map(
        shards, mesh=mesh, in_specs=placed, out_specs=(P("job", "col"), P("job")), check_vma=False
    )
```
